512 devices in a mesh: lat: 32 (over z, core), tp: 16 (over x, y).
Axes of the slice: x: 4, y: 4, z: 16, core: 2. Of those that a mesh axis runs over, the one named last changes fastest.
Arguments:
- activations: bfloat16 [256, 3584], P(None, 'lat'), may hold values from -6 to 6
- indices: int32 [256, 64], replicated, may hold values from 0 to 65535
- w_enc: bfloat16 [3584, 65536], P(None, ('lat', 'tp')), may hold values from -0.09375 to 0.09375
- b_enc: float32 [65536], P(('lat', 'tp')), may hold values from -5 to 5
- w_dec: bfloat16 [65536, 3584], P(('lat', 'tp')), may hold values from -3 to 3
- b_dec: float32 [3584], P('lat'), may hold values from -3 to 3
- w_gate: bfloat16 [3584, 14336], P('lat', 'tp'), may hold values from -0.09375 to 0.09375
- w_up: bfloat16 [3584, 14336], P('lat', 'tp'), may hold values from -0.09375 to 0.09375
- w_down: bfloat16 [14336, 3584], P('tp', 'lat'), may hold values from -0.046875 to 0.046875
- cotangent: bfloat16 [256, 3584], P(None, 'lat'), may hold values from -6 to 6
Outputs:
- output: bfloat16 [256, 3584], P('tp', 'lat')
- grad_enc: bfloat16 [3584, 65536], P(None, ('lat', 'tp'))
- grad_enc_bias: float32 [65536], P(('lat', 'tp'))
- grad_dec: bfloat16 [65536, 3584], P(('lat', 'tp'))
- grad_dec_bias: float32 [3584], P('lat')
The draws below stay inside these ranges and needn't reach their ends.
Inputs may be any that keep to these rules, and one draw needn't show every extreme that they name: `indices`: each row names 64 latents; a latent named more than once in a row counts once; some latents are named far more often than others.
All inputs are finite; a program needn't handle non-finite values.
Results may differ from the reference program's by a relative error of at most 0.011.
Values may be sent and summed in bfloat16 or wider, within the bound.
A program may use at most 64 MiB of HBM per device.

```python
import math
import jax
import jax.numpy as jnp
import numpy as np

D = 3584
FF = 14336
K = 64
ROWS = 256
LATENTS = 65536


def set_ends(result, own_key, least, top_value):
    index_at = [jax.random.randint(jax.random.fold_in(own_key, axis), (), 0, length) for axis, length in enumerate(result.shape)]
    widest = result.shape.index(max(result.shape))
    neighbour = index_at[:widest] + [(index_at[widest] + 1) % result.shape[widest]] + index_at[widest + 1:]
    return result.at[tuple(index_at)].set(least).at[tuple(neighbour)].set(top_value)


def strengthened(result, own_key, source, target, parts, factor):
    def block_of(axis_at):
        return (jnp.arange(result.shape[axis_at]) // (result.shape[axis_at] // parts)).reshape((-1,) + (1,) * (result.ndim - 1 - axis_at))

    one_side = jax.random.permutation(own_key, parts)[block_of(target)]
    far = (block_of(target) + parts // 2) % parts
    return jnp.where((block_of(source) == one_side) | (block_of(source) == far), factor * result, result)


def level_of(own_key, shape, split, least, largest):
    def one(dim, parts):
        heights = jax.random.uniform(jax.random.fold_in(jax.random.fold_in(own_key, 6), dim), (parts,), jnp.float32, least / len(split), largest / len(split))
        return jnp.repeat(jnp.exp(heights), shape[dim] // parts).reshape((-1,) + (1,) * (len(shape) - dim - 1))

    level = one(*split[0])
    for cut in split[1:]:
        level = level * one(*cut)
    return level


def rank_bounds(count, skew):
    portions = [(1 << 20) // math.isqrt(rank ** skew) + 1 for rank in range(1, count + 1)]
    deviation = 1 + sum(portions) // (1 << 30)
    return np.cumsum(np.array([max(1, weight // deviation) for weight in portions]))


def ranked_ids(rng, shape, number_of, skew):
    table = rank_bounds(number_of, skew)
    pick = jax.random.randint(jax.random.fold_in(rng, 1), shape, 0, int(table[number_of - 1]))
    standing = jnp.searchsorted(jnp.asarray(table, jnp.int32), pick, side="right")
    return jax.random.permutation(jax.random.fold_in(rng, 2), number_of)[standing].astype(jnp.int32)


def centred(stream_key, shape, deviation, bound, pieces=(), held_as=jnp.bfloat16):
    array = jax.random.normal(stream_key, shape, jnp.float32) * deviation
    if len(pieces) > 0:
        array = level_of(stream_key, shape, pieces, -0.22, 0.18) * array
    return jnp.clip(array, min=-bound, max=bound).astype(held_as)


def bell_draw_with(rng, shape, deviation, most, cuts, heavy, kind=jnp.bfloat16):
    array = deviation * jax.random.normal(rng, shape, jnp.float32)
    if cuts:
        array = array * level_of(rng, shape, cuts, -0.22, 0.18)
    return jnp.clip(strengthened(array, jax.random.fold_in(rng, 3), *heavy), -most, most).astype(kind)


def setup_inputs(seed: int = 0) -> dict:
    keys = jax.random.split(jax.random.key(seed), 11)
    activations = centred(keys[0], (ROWS, D), 1.0, 6.0, ((1, 32),))
    indices = set_ends(ranked_ids(keys[1], (ROWS, K), LATENTS, 2), jax.random.fold_in(keys[1], 3), 0, LATENTS - 1).astype(jnp.int32)
    w_enc = centred(keys[2], (D, LATENTS), D ** -0.5, 0.09375, ((1, 512),))
    b_enc = centred(keys[3], (LATENTS,), 1.0, 5.0, ((0, 512),), jnp.float32)
    w_dec = bell_draw_with(keys[4], (LATENTS, D), K ** -0.5, 3.0, ((0, 512),), (0, 1, 512, 6.0))
    b_dec = centred(keys[5], (D,), 0.5, 3.0, ((0, 32),), jnp.float32)
    w_gate = centred(keys[6], (D, FF), D ** -0.5, 0.09375, ((0, 32), (1, 16)))
    w_up = centred(keys[7], (D, FF), D ** -0.5, 0.09375, ((0, 32), (1, 16)))
    w_down = centred(keys[8], (FF, D), FF ** -0.5, 0.046875, ((0, 16), (1, 32)))
    cotangent = centred(keys[9], (ROWS, D), 1.0, 6.0, ((1, 32),))
    return dict(activations=activations, indices=indices, w_enc=w_enc, b_enc=b_enc, w_dec=w_dec, b_dec=b_dec, w_gate=w_gate, w_up=w_up, w_down=w_down, cotangent=cotangent)


def gelu_parts(value):
    coeff = 0.7978845608028654
    inner = coeff * (value + 0.044715 * value * value * value)
    tanh_term = jnp.tanh(inner)
    gelu_value = 0.5 * value * (1.0 + tanh_term)
    slope = 0.5 * (1.0 + tanh_term) + 0.5 * value * (1.0 - tanh_term * tanh_term) * coeff * (1.0 + 3.0 * 0.044715 * value * value)
    return gelu_value, slope


def reference(activations, indices, w_enc, b_enc, w_dec, b_dec, w_gate, w_up, w_down, cotangent):
    row_ids = jnp.arange(ROWS, dtype=jnp.int32)[:, None]
    hit = jnp.zeros((ROWS, LATENTS), jnp.float32).at[row_ids, indices].set(1.0)
    pre = jnp.dot(activations, w_enc, preferred_element_type=jnp.float32) + b_enc
    act = (pre * hit).astype(jnp.bfloat16)
    recon = (jnp.dot(act, w_dec, preferred_element_type=jnp.float32) + b_dec).astype(jnp.bfloat16)
    gate = jnp.dot(recon, w_gate, preferred_element_type=jnp.float32)
    up = jnp.dot(recon, w_up, preferred_element_type=jnp.float32)
    gelu_value, slope = gelu_parts(gate)
    hidden = (gelu_value * up).astype(jnp.bfloat16)
    output = (recon.astype(jnp.float32) + jnp.dot(hidden, w_down, preferred_element_type=jnp.float32)).astype(jnp.bfloat16)
    back_hidden = jnp.dot(cotangent, w_down.T, preferred_element_type=jnp.float32)
    back_gate = (back_hidden * up * slope).astype(jnp.bfloat16)
    back_up = (back_hidden * gelu_value).astype(jnp.bfloat16)
    through = jnp.dot(back_gate, w_gate.T, preferred_element_type=jnp.float32) + jnp.dot(back_up, w_up.T, preferred_element_type=jnp.float32)
    back_recon = (cotangent.astype(jnp.float32) + through + recon.astype(jnp.float32) - activations.astype(jnp.float32)).astype(jnp.bfloat16)
    back_act = (jnp.dot(back_recon, w_dec.T, preferred_element_type=jnp.float32) * hit).astype(jnp.bfloat16)
    grad_dec = jnp.dot(act.T, back_recon, preferred_element_type=jnp.float32).astype(jnp.bfloat16)
    grad_dec_bias = jnp.sum(back_recon.astype(jnp.float32), axis=0)
    grad_enc = jnp.dot(activations.T, back_act, preferred_element_type=jnp.float32).astype(jnp.bfloat16)
    grad_enc_bias = jnp.sum(back_act.astype(jnp.float32), axis=0)
    return (output, grad_enc, grad_enc_bias, grad_dec, grad_dec_bias)
```

```python
import functools

import jax
import jax.numpy as jnp
from jax import lax
from jax.experimental import pallas as pl
from jax.experimental.pallas import tpu as pltpu
from jax.sharding import PartitionSpec as P

MESH = pl.DeviceIdType.MESH
NZ = 16
NT = 16
PAIR = 1
MEM = 2 * PAIR
NP = NZ // PAIR
TB = NT // MEM
RB = 16 * TB
W = 112
FF = 896
BF = jnp.bfloat16
F32 = jnp.float32


def mm(a, b):
    return lax.dot_general(a, b, (((1,), (0,)), ((), ())), preferred_element_type=F32)


def mm_nt(a, b):
    return lax.dot_general(a, b, (((1,), (1,)), ((), ())), preferred_element_type=F32)


def mm_tn(a, b):
    return lax.dot_general(a, b, (((0,), (0,)), ((), ())), preferred_element_type=F32)


def gelu_parts(value):
    coeff = 0.7978845608028654
    inner = coeff * (value + 0.044715 * value * value * value)
    tanh_term = jnp.tanh(inner)
    gelu_value = 0.5 * value * (1.0 + tanh_term)
    slope = 0.5 * (1.0 + tanh_term) + 0.5 * value * (1.0 - tanh_term * tanh_term) * coeff * (
        1.0 + 3.0 * 0.044715 * value * value
    )
    return gelu_value, slope


def far_first(k, n):
    half = n // 2
    return half + ((k + 1) // 2) * (1 - 2 * lax.rem(k, 2))


def loop(n, body):
    def step(k, carry):
        body(k)
        return carry

    lax.fori_loop(0, n, step, 0)


def kernel(
    a_ref, idx_ref, wenc_ref, benc_ref, wdec_ref, bdec_ref, wg_ref, wu_ref, wn_ref, cot_ref,
    out_ref, genc_ref, gencb_ref, gdec_ref, gdecb_ref,
    apad, cpad, X, Y, WE, WD, hit, act, acc, SB, SR, PO, S2, R2, S3, R3, rc16, RC,
    WG, WU, WN, CT, BS, BR, BG, CS, CR, AG, DS, DR, HID, BGT, BUP, BH,
    s_s, s_r, z_s, z_r, t_s, t_r, g_s, g_r,
):
    lat = lax.axis_index("lat")
    tp = lax.axis_index("tp")
    z = lat // 2
    c = lax.rem(lat, 2)
    p = lat // MEM
    m = lax.rem(lat, MEM)
    oc = 1 - c
    sister = lat + 1 - 2 * c

    def copy(src, dst, ss, rs, dl, dt):
        return pltpu.make_async_remote_copy(
            src_ref=src, dst_ref=dst, send_sem=ss, recv_sem=rs, device_id=(dl, dt), device_id_type=MESH
        )

    bar = pltpu.get_barrier_semaphore()

    def hello_z(k):
        d = far_first(k, NZ)
        pl.semaphore_signal(bar, inc=1, device_id=(2 * lax.rem(z + d, NZ) + c, tp), device_id_type=MESH)

    def hello_t(k):
        kk = k + 1
        mm_ = lax.rem(m + kk // NT, MEM)
        tt = lax.rem(tp + lax.rem(kk, NT), NT)
        pl.semaphore_signal(bar, inc=1, device_id=(MEM * p + mm_, tt), device_id_type=MESH)

    loop(NZ - 1, hello_z)
    loop(MEM * NT - 1, hello_t)

    apad[...] = jnp.zeros_like(apad)
    cpad[...] = jnp.zeros_like(cpad)
    apad[:, :, :W] = a_ref[...].reshape(NT, 16, W)
    cpad[:, :, :W] = cot_ref[...].reshape(NT, 16, W)
    X[c, tp, z] = apad[tp]
    WG[m, :W] = wg_ref[...]
    WU[m, :W] = wu_ref[...]
    WN[m] = jnp.zeros((FF, 128), BF)
    WN[m, :, :W] = wn_ref[...]

    def pad_w(g):
        WG[g, W:] = jnp.zeros((128 - W, FF), BF)
        WU[g, W:] = jnp.zeros((128 - W, FF), BF)

    loop(MEM, pad_w)
    CT[m] = cpad[pl.ds(m * TB, TB)]

    pl.semaphore_wait(bar, NZ - 1 + MEM * NT - 1)

    class Gather:
        def __init__(self, buf, n):
            self.buf, self.n = buf, n

        def zcopy(self, d):
            to = lax.rem(z + d, NZ)
            return copy(self.buf.at[c, tp, z], self.buf.at[c, tp, z], z_s.at[self.n, to], z_r.at[self.n, z],
                        2 * to + c, tp)

        def zrecv(self, d):
            fr = lax.rem(z + d, NZ)
            return copy(self.buf.at[c, tp, fr], self.buf.at[c, tp, fr], z_s.at[self.n, fr], z_r.at[self.n, fr],
                        2 * fr + c, tp)

        def tcopy(self, d):
            to = lax.rem(tp + d, NT)
            return copy(self.buf.at[c, tp], self.buf.at[c, tp], t_s.at[self.n, to], t_r.at[self.n, tp], lat, to)

        def trecv(self, d):
            fr = lax.rem(tp + d, NT)
            return copy(self.buf.at[c, fr], self.buf.at[c, fr], t_s.at[self.n, fr], t_r.at[self.n, fr], lat, fr)

        def sis(self, which):
            return copy(self.buf.at[which], self.buf.at[which], s_s.at[self.n], s_r.at[self.n], sister, tp)

        def start_z(self):
            loop(NZ - 1, lambda k: self.zcopy(far_first(k, NZ)).start())

        def z_to_t(self):
            loop(NZ - 1, lambda k: self.zrecv(k + 1).wait_recv())
            loop(NT - 1, lambda k: self.tcopy(k + 1).start())

        def t_to_s(self):
            loop(NT - 1, lambda k: self.trecv(k + 1).wait_recv())
            self.sis(c).start()

        def done(self):
            self.sis(oc).wait_recv()

        def drain(self):
            loop(NZ - 1, lambda k: self.zcopy(k + 1).wait_send())
            loop(NT - 1, lambda k: self.tcopy(k + 1).wait_send())
            self.sis(c).wait_send()

    ga = Gather(X, 0)
    ga.start_z()

    def group_copies(k, own):
        d = k + 1
        mo = lax.rem(m + d, MEM)
        to = MEM * p + mo
        i = m if own else mo
        sem = mo if own else m
        ss, rs = g_s, g_r
        rows = pl.ds(mo * TB, TB)
        src = cpad.at[rows] if own else CT.at[i]
        return [
            copy(src, CT.at[i], ss.at[0, mo], rs.at[0, i], to, tp),
            copy(WN.at[i], WN.at[i], ss.at[1, mo], rs.at[1, i], to, tp),
            copy(WG.at[i, pl.ds(0, W)], WG.at[i, pl.ds(0, W)], ss.at[2, mo], rs.at[2, i], to, tp),
            copy(WU.at[i, pl.ds(0, W)], WU.at[i, pl.ds(0, W)], ss.at[3, mo], rs.at[3, i], to, tp),
        ]

    def start_group(k):
        for cp in group_copies(k, True):
            cp.start()

    loop(MEM - 1, start_group)

    def pad_enc(i):
        blk = wenc_ref[pl.ds(pl.multiple_of(i * W, 16), W), :]
        WE[lax.rem(i, 2), i // 2, :W] = blk
        WE[lax.rem(i, 2), i // 2, W:] = jnp.zeros((128 - W, 128), BF)

    loop(2 * NZ, pad_enc)
    for i in range(2 * NZ):
        WD[i % 2, i // 2] = jnp.zeros((128, 128), BF)
        WD[i % 2, i // 2, :, :W] = wdec_ref[:, i * W:(i + 1) * W]

    cols = (lat * NT + tp) * 128 + lax.broadcasted_iota(jnp.int32, (16, 128), 1)

    def hits(i):
        rows = pl.ds(pl.multiple_of(i * 16, 16), 16)
        ids = idx_ref[rows, :]
        found = jnp.zeros((16, 128), F32)
        for j in range(ids.shape[1]):
            found = jnp.where(ids[:, j:j + 1] == cols, 1.0, found)
        hit[rows, :] = found

    loop(NT, hits)

    ga.z_to_t()

    for k in range(MEM - 1):
        for cp in group_copies(k, False):
            cp.wait_recv()
    bh = mm_nt(CT[0].reshape(RB, 128), WN[0])
    for g in range(1, MEM):
        bh = bh + mm_nt(CT[g].reshape(RB, 128), WN[g])
    BS[...] = bh.reshape(NP, 8, FF)

    def ring(src, dst, n, own_src, send, d):
        q = lax.rem(p + d, NP)
        if send:
            return copy(src.at[q] if own_src else src, dst.at[p], z_s.at[n, q], z_r.at[n, p], MEM * q + m, tp)
        return copy(dst.at[q], dst.at[q], z_s.at[n, q], z_r.at[n, q], MEM * q + m, tp)

    def ring_start(src, dst, n, own_src):
        loop(NP - 1, lambda k: ring(src, dst, n, own_src, True, far_first(k, NP)).start())

    def ring_wait(src, dst, n, own_src):
        loop(NP - 1, lambda k: ring(src, dst, n, own_src, False, k + 1).wait_recv())

    def ring_drain(src, dst, n, own_src):
        loop(NP - 1, lambda k: ring(src, dst, n, own_src, True, k + 1).wait_send())

    BR[p] = BS[p]
    ring_start(BS, BR, 2, True)

    ga.t_to_s()

    def pre_half(h):
        def step(i, s):
            lhs = jnp.concatenate([X[h, :, 2 * i].reshape(256, 128), X[h, :, 2 * i + 1].reshape(256, 128)], axis=1)
            return s + mm(lhs, WE[h, pl.ds(2 * i, 2)].reshape(256, 128))

        acc[...] = lax.fori_loop(0, NZ // 2, step, acc[...])

    acc[...] = jnp.broadcast_to(benc_ref[...], (256, 128))
    pre_half(c)
    ga.done()
    pre_half(oc)
    act[...] = (acc[...] * hit[...]).astype(BF)

    def sis2(h):
        part = pl.ds(h * (NZ // 4), NZ // 4)
        return copy(SB.at[part], SR.at[part], s_s.at[2 + h], s_r.at[2 + h], sister, tp)

    def other(i):
        SB[i] = mm(act[...], WD[oc, i]).astype(BF).reshape(NT, 16, 128)

    for h in range(4):
        loop(NZ // 4, lambda k: other(h * (NZ // 4) + k))
        sis2(h).start()

    def own(i):
        PO[i] = mm(act[...], WD[c, i])

    loop(NZ, own)

    def both(i):
        S2[:, i] = (PO[i] + SR[i].reshape(256, 128).astype(F32)).astype(BF).reshape(NT, 16, 128)

    for h in range(4):
        sis2(h).wait_recv()
        loop(NZ // 4, lambda k: both(h * (NZ // 4) + k))

    def tsum(d, send):
        o = lax.rem(tp + d, NT)
        if send:
            return copy(S2.at[o], R2.at[tp], t_s.at[2, o], t_r.at[2, tp], lat, o)
        return copy(R2.at[o], R2.at[o], t_s.at[2, o], t_r.at[2, o], lat, o)

    loop(NT - 1, lambda k: tsum(k + 1, True).start())
    R2[tp] = S2[tp]

    ring_wait(BS, BR, 2, True)
    BG[p] = jnp.sum(BR[...], axis=0)
    ring_start(BG.at[p], BG, 3, False)

    loop(NT - 1, lambda k: tsum(k + 1, False).wait_recv())

    def tadd(i):
        S3[i] = jnp.sum(R2[:, i].astype(F32), axis=0).astype(BF)

    loop(NZ, tadd)

    def zsum(d, send):
        o = lax.rem(z + d, NZ)
        if send:
            return copy(S3.at[o], R3.at[z], z_s.at[4, o], z_r.at[4, z], 2 * o + c, tp)
        return copy(R3.at[o], R3.at[o], z_s.at[4, o], z_r.at[4, o], 2 * o + c, tp)

    loop(NZ - 1, lambda k: zsum(far_first(k, NZ), True).start())
    R3[z] = S3[z]
    loop(NZ - 1, lambda k: zsum(k + 1, False).wait_recv())
    rc16[...] = (jnp.sum(R3[...].astype(F32), axis=0) + bdec_ref[...]).astype(BF)

    mt = tp // TB
    slot = lax.rem(tp, TB)

    def rcopy(d):
        o = lax.rem(tp + d, NT)
        return copy(rc16, RC.at[m, slot], t_s.at[3, o], t_r.at[3, m * TB + slot], MEM * p + mt, o)

    def rwait(k):
        g = k // TB
        i = lax.rem(k, TB)

        @pl.when(jnp.logical_or(g != m, m * TB + i != tp))
        def _():
            copy(rc16, RC.at[g, i], t_s.at[3, 0], t_r.at[3, k], MEM * p + g, m * TB + i).wait_recv()

    loop(NT - 1, lambda k: rcopy(k + 1).start())

    @pl.when(mt == m)
    def _():
        RC[m, slot] = rc16[...]

    @pl.when(mt != m)
    def _():
        rcopy(0).start()

    loop(MEM * TB, rwait)

    def pairs(i):
        return jnp.concatenate([RC[2 * i].reshape(RB, 128), RC[2 * i + 1].reshape(RB, 128)], axis=1)

    gate = mm(pairs(0), WG[0:2].reshape(256, FF))
    up = mm(pairs(0), WU[0:2].reshape(256, FF))
    for i in range(1, MEM // 2):
        gate = gate + mm(pairs(i), WG[2 * i:2 * i + 2].reshape(256, FF))
        up = up + mm(pairs(i), WU[2 * i:2 * i + 2].reshape(256, FF))
    CS[:, 0:16, :] = jnp.concatenate([gate.reshape(NP, 8, FF), up.reshape(NP, 8, FF)], axis=1).astype(BF)
    ring_start(CS, CR, 5, True)
    CR[p] = CS[p]
    ring_wait(CS, CR, 5, True)
    AG[p] = jnp.sum(CR[...].astype(F32), axis=0).astype(BF)
    ring_start(AG.at[p], AG, 6, False)
    ring_wait(BG.at[p], BG, 3, False)
    ring_wait(AG.at[p], AG, 6, False)

    def cells(i):
        both_ = AG[i].astype(F32)
        gate_, up_ = both_[:8], both_[8:]
        bh_ = BG[i]
        gelu_value, slope = gelu_parts(gate_)
        HID[i] = gelu_value * up_
        BGT[i] = bh_ * up_ * slope
        BUP[i] = bh_ * gelu_value

    loop(NP, cells)
    hidden = HID[...].reshape(RB, FF).astype(BF)
    bgate = BGT[...].reshape(RB, FF).astype(BF)
    bup = BUP[...].reshape(RB, FF).astype(BF)
    for g in range(MEM):
        DS[g, :, 0] = mm(hidden, WN[g]).astype(BF).reshape(TB, 16, 128)
        DS[g, :, 1] = (mm_nt(bgate, WG[g]) + mm_nt(bup, WU[g])).astype(BF).reshape(TB, 16, 128)

    def dcopy(k):
        g = k // TB
        i = lax.rem(k, TB)
        return copy(DS.at[g, i], DR.at[tp], t_s.at[4, k], t_r.at[4, tp], MEM * p + g, m * TB + i)

    def unless_self(k, fn):
        g = k // TB
        i = lax.rem(k, TB)

        @pl.when(jnp.logical_or(g != m, m * TB + i != tp))
        def _():
            fn(k)

    def dwait(d):
        o = lax.rem(tp + d, NT)
        copy(DR.at[o], DR.at[o], t_s.at[4, 0], t_r.at[4, o], MEM * p + mt, o).wait_recv()

    loop(MEM * TB, lambda k: unless_self(k, lambda kk: dcopy(kk).start()))

    @pl.when(mt == m)
    def _():
        DR[tp] = DS[m, slot]

    @pl.when(mt != m)
    def _():
        dwait(0)

    loop(NT - 1, lambda k: dwait(k + 1))
    sums = jnp.sum(DR[...].astype(F32), axis=0)
    recon = rc16[...].astype(F32)
    out_ref[...] = (recon + sums[0]).astype(BF)[:, :W]
    back = cpad[tp].astype(F32) + sums[1] + recon - apad[tp].astype(F32)
    Y[c, tp, z] = back.astype(BF)

    gy = Gather(Y, 1)
    gy.start_z()
    gy.z_to_t()
    gy.t_to_s()

    def back_half(h):
        def step(i, s):
            y = Y[h, :, i].reshape(256, 128)
            gdec_ref[2 * i + h] = mm_tn(act[...], y).astype(BF)
            return s + mm_nt(y, WD[h, i])

        acc[...] = lax.fori_loop(0, NZ, step, acc[...])

    acc[...] = jnp.zeros_like(acc)
    back_half(c)
    gdecb_ref[...] = jnp.sum(Y[c, :, z].reshape(256, 128).astype(F32), axis=0, keepdims=True)
    gy.done()
    back_half(oc)
    bact = (acc[...] * hit[...]).astype(BF)
    gencb_ref[...] = jnp.sum(bact.astype(F32), axis=0, keepdims=True)
    act[...] = bact

    def enc_grad(i):
        x = X[lax.rem(i, 2), :, i // 2].reshape(256, 128)
        genc_ref[pl.ds(pl.multiple_of(i * W, 16), W), :] = mm_tn(x, act[...])[:W].astype(BF)

    loop(2 * NZ, enc_grad)

    ga.drain()
    gy.drain()

    def drain_group(k):
        for cp in group_copies(k, True):
            cp.wait_send()

    loop(MEM - 1, drain_group)
    ring_drain(BS, BR, 2, True)
    ring_drain(BG.at[p], BG, 3, False)
    ring_drain(CS, CR, 5, True)
    ring_drain(AG.at[p], AG, 6, False)
    for h in range(4):
        sis2(h).wait_send()
    loop(NT - 1, lambda k: tsum(k + 1, True).wait_send())
    loop(NZ - 1, lambda k: zsum(k + 1, True).wait_send())
    loop(NT - 1, lambda k: rcopy(k + 1).wait_send())

    @pl.when(mt != m)
    def _():
        rcopy(0).wait_send()

    loop(MEM * TB, lambda k: unless_self(k, lambda kk: dcopy(kk).wait_send()))


def on_device(activations, indices, w_enc, b_enc, w_dec, b_dec, w_gate, w_up, w_down, cotangent):
    vm = pltpu.VMEM
    dma = pltpu.SemaphoreType.DMA
    out, genc, gencb, gdec, gdecb = pl.pallas_call(
        kernel,
        out_shape=(
            jax.ShapeDtypeStruct((16, W), BF),
            jax.ShapeDtypeStruct((2 * NZ * W, 128), BF),
            jax.ShapeDtypeStruct((1, 128), F32),
            jax.ShapeDtypeStruct((2 * NZ, 128, 128), BF),
            jax.ShapeDtypeStruct((1, 128), F32),
        ),
        in_specs=[pl.BlockSpec(memory_space=pltpu.VMEM)] * 10,
        out_specs=[pl.BlockSpec(memory_space=pltpu.VMEM)] * 5,
        scratch_shapes=[
            vm((NT, 16, 128), BF),
            vm((NT, 16, 128), BF),
            vm((2, NT, NZ, 16, 128), BF),
            vm((2, NT, NZ, 16, 128), BF),
            vm((2, NZ, 128, 128), BF),
            vm((2, NZ, 128, 128), BF),
            vm((256, 128), F32),
            vm((256, 128), BF),
            vm((256, 128), F32),
            vm((NZ, NT, 16, 128), BF),
            vm((NZ, NT, 16, 128), BF),
            vm((NZ, 256, 128), F32),
            vm((NT, NZ, 16, 128), BF),
            vm((NT, NZ, 16, 128), BF),
            vm((NZ, 16, 128), BF),
            vm((NZ, 16, 128), BF),
            vm((16, 128), BF),
            vm((MEM, TB, 16, 128), BF),
            vm((MEM, 128, FF), BF),
            vm((MEM, 128, FF), BF),
            vm((MEM, FF, 128), BF),
            vm((MEM, TB, 16, 128), BF),
            vm((NP, 8, FF), F32),
            vm((NP, 8, FF), F32),
            vm((NP, 8, FF), F32),
            vm((NP, 16, FF), BF),
            vm((NP, 16, FF), BF),
            vm((NP, 16, FF), BF),
            vm((MEM, TB, 2, 16, 128), BF),
            vm((NT, 2, 16, 128), BF),
            vm((NP, 8, FF), F32),
            vm((NP, 8, FF), F32),
            vm((NP, 8, FF), F32),
            vm((8, 128), F32),
            dma((6,)), dma((6,)),
            dma((7, NZ)), dma((7, NZ)),
            dma((5, NT)), dma((5, NT)),
            dma((4, MEM)), dma((4, MEM)),
        ],
        compiler_params=pltpu.CompilerParams(
            collective_id=1, has_side_effects=True, vmem_limit_bytes=56 * 2**20
        ),
        cost_estimate=pl.CostEstimate(flops=2 * 10**9, bytes_accessed=6 * 10**6, transcendentals=10**5),
        name="sae_step",
    )(
        activations, indices, w_enc, b_enc.reshape(1, 128), w_dec, jnp.pad(b_dec, (0, 128 - W)).reshape(1, 128),
        w_gate, w_up, w_down, cotangent,
    )
    gdec = gdec[:, :, :W].transpose(1, 0, 2).reshape(128, 2 * NZ * W)
    return out, genc, gencb.reshape(128), gdec, gdecb[0, :W]


def solution(mesh):
    return jax.shard_map(
        on_device,
        mesh=mesh,
        in_specs=(
            P(None, "lat"),
            P(),
            P(None, ("lat", "tp")),
            P(("lat", "tp")),
            P(("lat", "tp"), None),
            P("lat"),
            P("lat", "tp"),
            P("lat", "tp"),
            P("tp", "lat"),
            P(None, "lat"),
        ),
        out_specs=(
            P("tp", "lat"),
            P(None, ("lat", "tp")),
            P(("lat", "tp")),
            P(("lat", "tp"), None),
            P("lat"),
        ),
        check_vma=False,
    )
```

```python
import functools

import jax
import jax.numpy as jnp
from jax import lax
from jax.experimental import pallas as pl
from jax.experimental.pallas import tpu as pltpu
from jax.sharding import PartitionSpec as P

MESH = pl.DeviceIdType.MESH
NZ = 16
NT = 16
PAIR = 2
MEM = 2 * PAIR
NP = NZ // PAIR
TB = NT // MEM
RB = 16 * TB
W = 112
FF = 896
NEAR = 9
BF = jnp.bfloat16
F32 = jnp.float32


def mm(a, b):
    return lax.dot_general(a, b, (((1,), (0,)), ((), ())), preferred_element_type=F32)


def mm_nt(a, b):
    return lax.dot_general(a, b, (((1,), (1,)), ((), ())), preferred_element_type=F32)


def gelu_parts(value):
    coeff = 0.7978845608028654
    inner = coeff * (value + 0.044715 * value * value * value)
    tanh_term = jnp.tanh(inner)
    gelu_value = 0.5 * value * (1.0 + tanh_term)
    slope = 0.5 * (1.0 + tanh_term) + 0.5 * value * (1.0 - tanh_term * tanh_term) * coeff * (
        1.0 + 3.0 * 0.044715 * value * value
    )
    return gelu_value, slope


def offset(s):
    return (s + 1) // 2 * (2 * lax.rem(s, 2) - 1)


def mirror(s):
    return jnp.where(jnp.logical_or(s == 0, s == NZ - 1), s, s + 2 * lax.rem(s, 2) - 1)


def slot_of(d):
    d = lax.rem(d + NZ, NZ)
    return jnp.maximum(jnp.where(d <= NZ // 2, 2 * d - 1, 2 * (NZ - d)), 0)


def loop(n, body, start=0):
    def step(k, carry):
        body(k)
        return carry

    lax.fori_loop(start, n, step, 0)


def kernel(
    stop,
    at_ref, idxt_ref, wenc_ref, benc_ref, wdec_ref, bdec_ref, wg_ref, wu_ref, wnt_ref, cott_ref,
    out_ref, genc_ref, gencb_ref, gdec_ref, gdecb_ref,
    apad, cpad, ZA, ZB, X, Y, XT, WE, WD, WDT, hit, hit2, bias2, act, actf, actt, acc, S2, R2, S3, R3, rc16, RC,
    WG, WU, WGT, WUT, WN, CT, BS, BR, BG, CS, CR, AG, DS, DR, HID, BGT, BUP, wdec, wnt,
    s_s, s_r, z_s, z_r, t_s, t_r, g_s, g_r, l_s,
):
    lat = lax.axis_index("lat")
    tp = lax.axis_index("tp")
    z = lat // 2
    c = lax.rem(lat, 2)
    p = lat // MEM
    m = lax.rem(lat, MEM)
    oc = 1 - c
    sister = lat + 1 - 2 * c
    partner = MEM * p + lax.rem(m + 2, MEM)
    drains = []
    comes = {}

    def finish():
        for wait in comes.values():
            wait()
        for wait in drains:
            wait()

    def got(name):
        comes.pop(name)()

    def copy(src, dst, ss, rs, dl, dt):
        return pltpu.make_async_remote_copy(
            src_ref=src, dst_ref=dst, send_sem=ss, recv_sem=rs, device_id=(dl, dt), device_id_type=MESH
        )

    def to_sister(src, dst, n):
        return copy(src, dst, s_s.at[n], s_r.at[n], sister, tp)

    def z_at(s):
        return lax.rem(z + offset(s) + NZ, NZ)

    bar = pltpu.get_barrier_semaphore()

    def hello_z(k):
        pl.semaphore_signal(bar, inc=1, device_id=(2 * z_at(NZ - 1 - k) + c, tp), device_id_type=MESH)

    def hello_t(k):
        kk = k + 1
        mo = lax.rem(m + kk // NT, MEM)
        to = lax.rem(tp + lax.rem(kk, NT), NT)
        pl.semaphore_signal(bar, inc=1, device_id=(MEM * p + mo, to), device_id_type=MESH)

    loop(NZ - 1, hello_z)
    loop(MEM * NT - 1, hello_t)

    top = pl.ds(0, W)
    l_wnt = pltpu.make_async_copy(wnt_ref, wnt.at[top], l_s.at[0])
    l_wg = pltpu.make_async_copy(wg_ref, WG.at[m, top], l_s.at[1])
    l_wu = pltpu.make_async_copy(wu_ref, WU.at[m, top], l_s.at[2])
    l_wd = pltpu.make_async_copy(wdec_ref, wdec, l_s.at[3])

    def l_we(k):
        h = k // NZ
        s = lax.rem(k, NZ)
        rows = pl.ds(pl.multiple_of((2 * z_at(s) + h) * W, 16), W)
        return pltpu.make_async_copy(wenc_ref.at[rows], WE.at[c, s, h, top], l_s.at[4 + k])

    l_wnt.start()
    loop(2 * NZ, lambda k: l_we(k).start())
    l_wd.start()
    l_wg.start()
    l_wu.start()

    fill = jnp.zeros((128 - W, 256), BF)
    apad[...] = jnp.concatenate([at_ref[...], fill], axis=0).T.reshape(NT, 16, 128)
    cpad[...] = jnp.concatenate([cott_ref[...], fill], axis=0).T.reshape(NT, 16, 128)
    ZA[0] = apad[tp]

    def pad_w(g):
        WG[g, W:] = jnp.zeros((128 - W, FF), BF)
        WU[g, W:] = jnp.zeros((128 - W, FF), BF)

    def pad_e(k):
        WE[c, k // 2, lax.rem(k, 2), W:] = jnp.zeros((128 - W, 128), BF)

    loop(MEM, pad_w)
    loop(2 * NZ, pad_e)
    wnt[W:] = jnp.zeros((128 - W, FF), BF)
    CT[m] = cpad[pl.ds(m * TB, TB)]
    l_wnt.wait()
    WN[m] = wnt[...].T

    pl.semaphore_wait(bar, NZ - 1 + MEM * NT - 1)
    if stop == 0:
        loop(2 * NZ, lambda k: l_we(k).wait())
        l_wg.wait()
        l_wu.wait()
        l_wd.wait()
        return finish()

    ht = tp // 8
    jt = lax.rem(tp, 8)

    class Gather:
        def __init__(self, zb, buf, n):
            self.zb, self.buf, self.n = zb, buf, n

        def z_out(self, s):
            r = mirror(s)
            return copy(self.zb.at[0], self.zb.at[r], z_s.at[self.n, s], z_r.at[self.n, r], 2 * z_at(s) + c, tp)

        def z_in(self, s):
            return copy(self.zb.at[s], self.zb.at[s], z_s.at[self.n, s], z_r.at[self.n, s], 2 * z_at(s) + c, tp)

        def rows(self, w):
            return pl.ds(0, NEAR) if w == 0 else pl.ds(NEAR, NZ - NEAR)

        def t_out(self, w, d):
            to = lax.rem(tp + d, NT)
            sem = 2 * self.n + w
            return copy(self.zb.at[self.rows(w)], self.buf.at[ht, jt, c, self.rows(w)],
                        t_s.at[sem, to], t_r.at[sem, c * 8 + jt], 2 * z + ht, to)

        def t_in(self, w, k):
            dst = self.buf.at[c, lax.rem(k, 8), k // 8, self.rows(w)]
            sem = 2 * self.n + w
            return copy(dst, dst, t_s.at[sem, 0], t_r.at[sem, k], 2 * z + k // 8, c * 8 + lax.rem(k, 8))

        def sis(self, which, w):
            part = self.buf.at[which, :, :, self.rows(w)]
            return to_sister(part, part, 2 * self.n + w)

        def start(self):
            loop(NZ - 1, lambda k: self.z_out(NZ - 1 - k).start())
            drains.append(lambda: loop(NZ, lambda s: self.z_out(s).wait_send(), 1))
            comes["z0"] = lambda: loop(NEAR, lambda s: self.z_in(s).wait_recv(), 1)
            comes["z1"] = lambda: loop(NZ, lambda s: self.z_in(s).wait_recv(), NEAR)

        def forward(self, w):
            got("z%d" % w)
            loop(NT, lambda d: self.t_out(w, d).start(), 1)

            @pl.when(ht != c)
            def _():
                self.t_out(w, 0).start()

            @pl.when(ht == c)
            def _():
                self.buf[c, jt, c, self.rows(w)] = self.zb[self.rows(w)]

            def drain():
                loop(NT, lambda d: self.t_out(w, d).wait_send(), 1)

                @pl.when(ht != c)
                def _():
                    self.t_out(w, 0).wait_send()

            def come(k):
                @pl.when(jnp.logical_or(k // 8 != c, c * 8 + lax.rem(k, 8) != tp))
                def _():
                    self.t_in(w, k).wait_recv()

            drains.append(drain)
            comes["t%d" % w] = lambda: loop(NT, come)

        def swap(self, w):
            self.sis(c, w).start()
            drains.append(lambda: self.sis(c, w).wait_send())
            comes["sis%d%d" % (self.n, w)] = lambda: self.sis(oc, w).wait_recv()

    ga = Gather(ZA, X, 0)
    ga.start()

    def weight(a, i):
        return [WN.at[i], WG.at[i, top], WU.at[i, top]][a]

    def share(a, i, to):
        return copy(weight(a, i), weight(a, i), g_s.at[a, i, 0 if to is sister else 1], g_r.at[a, i], to, tp)

    slot_p = lax.rem(m + 2, MEM)
    slot_s = m + 1 - 2 * c
    slot_sp = lax.rem(slot_s + 2, MEM)

    def share_out(a):
        share(a, m, sister).start()
        share(a, m, partner).start()
        drains.append(lambda: [share(a, m, sister).wait_send(), share(a, m, partner).wait_send()])
        comes["sis w%d" % a] = lambda: share(a, slot_s, sister).wait_recv()
        comes["chip w%d" % a] = lambda: share(a, slot_p, partner).wait_recv()

    def share_on(a):
        got("chip w%d" % a)
        share(a, slot_p, sister).start()
        drains.append(lambda: share(a, slot_p, sister).wait_send())
        comes["last w%d" % a] = lambda: share(a, slot_sp, sister).wait_recv()

    def cot_out(d):
        mo = lax.rem(m + d, MEM)
        return copy(cpad.at[pl.ds(mo * TB, TB)], CT.at[m], g_s.at[3, mo, 0], g_r.at[3, m], MEM * p + mo, tp)

    def cot_in(d):
        mo = lax.rem(m + d, MEM)
        return copy(CT.at[mo], CT.at[mo], g_s.at[3, mo, 0], g_r.at[3, mo], MEM * p + mo, tp)

    loop(MEM, lambda d: cot_out(d).start(), 1)
    drains.append(lambda: loop(MEM, lambda d: cot_out(d).wait_send(), 1))
    comes["cot"] = lambda: loop(MEM, lambda d: cot_in(d).wait_recv(), 1)
    share_out(0)

    ids_col = (lat * NT + tp) * 128 + lax.broadcasted_iota(jnp.int32, (128, 256), 0)

    def one_hit(j, found):
        return jnp.where(idxt_ref[pl.ds(j, 1), :] == ids_col, 1.0, found)

    hit[...] = lax.fori_loop(0, idxt_ref.shape[0], one_hit, jnp.zeros((128, 256), F32), unroll=8).T
    other_rows = pl.ds(pl.multiple_of(oc * 128, 128), 128)
    own_rows = pl.ds(pl.multiple_of(c * 128, 128), 128)
    hit2[c] = hit[own_rows, :]

    def hit_swap():
        return to_sister(hit.at[other_rows], hit2.at[c], 4)

    hit_swap().start()
    drains.append(lambda: hit_swap().wait_send())
    bias2[c] = jnp.broadcast_to(benc_ref[...], (8, 128))

    def bias_swap(i):
        return to_sister(bias2.at[i], bias2.at[i], 8)

    bias_swap(c).start()
    drains.append(lambda: bias_swap(c).wait_send())
    comes["bias"] = lambda: bias_swap(oc).wait_recv()
    comes["hit"] = lambda: to_sister(hit2.at[oc], hit2.at[oc], 4).wait_recv()

    loop(2 * NZ, lambda k: l_we(k).wait())

    def enc_swap(i):
        return to_sister(WE.at[i], WE.at[i], 5)

    enc_swap(c).start()
    drains.append(lambda: enc_swap(c).wait_send())
    comes["enc"] = lambda: enc_swap(oc).wait_recv()

    ga.forward(0)

    l_wd.wait()

    def dec_block(i):
        blk = jnp.concatenate([wdec[:, i * W:(i + 1) * W], jnp.zeros((128, 128 - W), BF)], axis=1)
        s = slot_of(i // 2 - z)
        WD[c, i % 2, s] = blk
        WDT[s, i % 2] = blk.T

    for i in range(NZ):
        dec_block(i)
    ga.forward(1)
    for i in range(NZ, 2 * NZ):
        dec_block(i)

    def dec_swap(i):
        return to_sister(WD.at[i], WD.at[i], 6)

    dec_swap(c).start()
    drains.append(lambda: dec_swap(c).wait_send())
    comes["dec"] = lambda: dec_swap(oc).wait_recv()
    l_wg.wait()
    l_wu.wait()
    share_out(1)
    share_out(2)
    share_on(0)
    if stop == 1:
        return finish()

    def ring(src, dst, n, own_src, send, d):
        q = lax.rem(p + d, NP)
        if send:
            return copy(src.at[q] if own_src else src, dst.at[p], z_s.at[n, q], z_r.at[n, p], MEM * q + m, tp)
        return copy(dst.at[q], dst.at[q], z_s.at[n, q], z_r.at[n, q], MEM * q + m, tp)

    def far(k):
        return NP // 2 + (k + 1) // 2 * (1 - 2 * lax.rem(k, 2))

    def ring_start(src, dst, n, own_src, name):
        loop(NP - 1, lambda k: ring(src, dst, n, own_src, True, far(k)).start())
        drains.append(lambda: loop(NP, lambda d: ring(src, dst, n, own_src, True, d).wait_send(), 1))
        comes[name] = lambda: loop(NP, lambda d: ring(src, dst, n, own_src, False, d).wait_recv(), 1)

    got("cot")
    got("sis w0")
    got("last w0")
    bh = mm_nt(CT[0].reshape(RB, 128), WN[0])
    for g in range(1, MEM):
        bh = bh + mm_nt(CT[g].reshape(RB, 128), WN[g])
    BS[...] = bh.reshape(NP, 8, FF)
    BR[p] = BS[p]
    ring_start(BS, BR, 2, True, "bh sum")
    if stop == 2:
        return finish()

    def pre_part(start, lo, hi):
        pre = start
        for i in range(lo, hi):
            lhs = jnp.concatenate([X[c, :, 0, i].reshape(128, 128), X[c, :, 1, i].reshape(128, 128)], axis=1)
            rhs = jnp.concatenate([WE[0, i].reshape(256, 128), WE[1, i].reshape(256, 128)], axis=1)
            pre = pre + mm(lhs, rhs)
        return pre

    got("bias")
    got("enc")
    got("hit")
    got("t0")
    ga.swap(0)
    pre = pre_part(jnp.concatenate([bias2[0, 0:1], bias2[1, 0:1]], axis=1), 0, NEAR)
    got("t1")
    ga.swap(1)
    pre = pre_part(pre, NEAR, NZ)
    act[...] = (pre * jnp.concatenate([hit2[0], hit2[1]], axis=1)).astype(BF)
    if stop == 3:
        return finish()

    got("dec")
    half = NZ // 2

    def tsum_out(w, k):
        rows = pl.ds(w * half, half)
        return copy(S2.at[lax.rem(k, 8), k // 8, rows], R2.at[tp, rows], t_s.at[4 + w, k], t_r.at[4 + w, tp],
                    2 * z + k // 8, c * 8 + lax.rem(k, 8))

    def tsum_in(w, o):
        rows = pl.ds(w * half, half)
        return copy(R2.at[o, rows], R2.at[o, rows], t_s.at[4 + w, o], t_r.at[4 + w, o], 2 * z + ht, o)

    def unless_me(k, fn):
        @pl.when(jnp.logical_or(k // 8 != c, c * 8 + lax.rem(k, 8) != tp))
        def _():
            fn()

    def tsum_come(w):
        loop(NT, lambda d: tsum_in(w, lax.rem(tp + d, NT)).wait_recv(), 1)

        @pl.when(ht != c)
        def _():
            tsum_in(w, tp).wait_recv()

    for w in (1, 0):
        for i in range(w * half, (w + 1) * half):
            rhs = jnp.concatenate([jnp.concatenate([WD[0, e, i], WD[1, e, i]], axis=0) for e in (0, 1)], axis=1)
            both = mm(act[...], rhs).astype(BF)
            S2[:, 0, i] = both[:, :128].reshape(8, 16, 128)
            S2[:, 1, i] = both[:, 128:].reshape(8, 16, 128)
        loop(NT, lambda k: unless_me(k, lambda: tsum_out(w, k).start()))

        @pl.when(ht == c)
        def _():
            rows = pl.ds(w * half, half)
            R2[tp, rows] = S2[jt, c, rows]

        drains.append(functools.partial(
            lambda w: loop(NT, lambda k: unless_me(k, lambda: tsum_out(w, k).wait_send())), w))
        comes["ts%d" % w] = functools.partial(tsum_come, w)
    if stop == 4:
        return finish()

    actf[c] = act[:, pl.ds(pl.multiple_of(c * 128, 128), 128)]

    def act_swap():
        return to_sister(act.at[:, pl.ds(pl.multiple_of(oc * 128, 128), 128)], actf.at[c], 7)

    act_swap().start()
    drains.append(lambda: act_swap().wait_send())
    comes["act"] = lambda: to_sister(actf.at[oc], actf.at[oc], 7).wait_recv()

    share_on(1)
    share_on(2)
    got("sis00")
    got("sis01")
    got("bh sum")
    BG[p] = jnp.sum(BR[...], axis=0)
    ring_start(BG.at[p], BG, 3, False, "bh")

    def z_out(s):
        r = mirror(s)
        return copy(S3.at[s], R3.at[r], z_s.at[4, s], z_r.at[4, r], 2 * z_at(s) + c, tp)

    def z_in(s):
        return copy(R3.at[s], R3.at[s], z_s.at[4, s], z_r.at[4, s], 2 * z_at(s) + c, tp)

    def tadd(s):
        S3[s] = jnp.sum(R2[:, s].astype(F32), axis=0).astype(BF)

    def far_sum(k):
        tadd(NZ - 1 - k)
        z_out(NZ - 1 - k).start()

    got("ts1")
    loop(half, far_sum)
    got("ts0")
    loop(half - 1, lambda k: far_sum(k + half))
    tadd(0)
    R3[0] = S3[0]
    drains.append(lambda: loop(NZ, lambda s: z_out(s).wait_send(), 1))
    comes["z sum"] = lambda: loop(NZ, lambda s: z_in(s).wait_recv(), 1)
    if stop == 5:
        return finish()
    for a in (1, 2):
        got("sis w%d" % a)
        got("last w%d" % a)
    for g in range(MEM):
        WGT[g] = WG[g].T
        WUT[g] = WU[g].T
    got("z sum")
    bias = jnp.concatenate([bdec_ref[...], jnp.zeros((1, 128 - W), F32)], axis=1)
    rc16[...] = (jnp.sum(R3[...].astype(F32), axis=0) + bias).astype(BF)
    if stop == 6:
        return finish()

    mt = tp // TB
    slot = lax.rem(tp, TB)

    def rcopy(d):
        o = lax.rem(tp + d, NT)
        return copy(rc16, RC.at[m, slot], t_s.at[6, o], t_r.at[6, m * TB + slot], MEM * p + mt, o)

    def unless_self(k, fn):
        g = k // TB
        i = lax.rem(k, TB)

        @pl.when(jnp.logical_or(g != m, m * TB + i != tp))
        def _():
            fn(k)

    def rwait(k):
        g = k // TB
        i = lax.rem(k, TB)
        copy(rc16, RC.at[g, i], t_s.at[6, 0], t_r.at[6, k], MEM * p + g, m * TB + i).wait_recv()

    loop(NT, lambda d: rcopy(d).start(), 1)

    @pl.when(mt == m)
    def _():
        RC[m, slot] = rc16[...]

    @pl.when(mt != m)
    def _():
        rcopy(0).start()

    def rdrain():
        loop(NT, lambda d: rcopy(d).wait_send(), 1)

        @pl.when(mt != m)
        def _():
            rcopy(0).wait_send()

    drains.append(rdrain)
    loop(MEM * TB, lambda k: unless_self(k, rwait))
    if stop == 7:
        return finish()

    def pairs(i):
        return jnp.concatenate([RC[2 * i].reshape(RB, 128), RC[2 * i + 1].reshape(RB, 128)], axis=1)

    gate = mm(pairs(0), WG[0:2].reshape(256, FF))
    up = mm(pairs(0), WU[0:2].reshape(256, FF))
    for i in range(1, MEM // 2):
        gate = gate + mm(pairs(i), WG[2 * i:2 * i + 2].reshape(256, FF))
        up = up + mm(pairs(i), WU[2 * i:2 * i + 2].reshape(256, FF))
    CS[...] = jnp.concatenate([gate.reshape(NP, 8, FF), up.reshape(NP, 8, FF)], axis=1).astype(BF)
    ring_start(CS, CR, 5, True, "gate sum")
    CR[p] = CS[p]
    for h in range(2):
        for i in range(NZ):
            XT[h, i] = X[:, :, h, i].reshape(256, 128).T
    got("act")
    actt[...] = actf[...].reshape(256, 128).T
    if stop == 8:
        return finish()
    got("gate sum")
    AG[p] = jnp.sum(CR[...].astype(F32), axis=0).astype(BF)
    ring_start(AG.at[p], AG, 6, False, "gate")
    got("bh")
    got("gate")
    if stop == 9:
        return finish()

    def cells(i):
        both_ = AG[i].astype(F32)
        gate_, up_ = both_[:8], both_[8:]
        bh_ = BG[i]
        gelu_value, slope = gelu_parts(gate_)
        HID[i] = gelu_value * up_
        BGT[i] = bh_ * up_ * slope
        BUP[i] = bh_ * gelu_value

    loop(NP, cells)
    hidden = HID[...].reshape(RB, FF).astype(BF)
    bgate = BGT[...].reshape(RB, FF).astype(BF)
    bup = BUP[...].reshape(RB, FF).astype(BF)
    for g in range(MEM):
        DS[g, :, 0] = mm(hidden, WN[g]).astype(BF).reshape(TB, 16, 128)
        DS[g, :, 1] = (mm(bgate, WGT[g]) + mm(bup, WUT[g])).astype(BF).reshape(TB, 16, 128)
    if stop == 10:
        return finish()

    def dcopy(k):
        g = k // TB
        i = lax.rem(k, TB)
        return copy(DS.at[g, i], DR.at[tp], t_s.at[7, k], t_r.at[7, tp], MEM * p + g, m * TB + i)

    def dwait(d):
        o = lax.rem(tp + d, NT)
        copy(DR.at[o], DR.at[o], t_s.at[7, 0], t_r.at[7, o], MEM * p + mt, o).wait_recv()

    loop(MEM * TB, lambda k: unless_self(k, lambda kk: dcopy(kk).start()))
    drains.append(lambda: loop(MEM * TB, lambda k: unless_self(k, lambda kk: dcopy(kk).wait_send())))

    @pl.when(mt == m)
    def _():
        DR[tp] = DS[m, slot]

    @pl.when(mt != m)
    def _():
        dwait(0)

    loop(NT, dwait, 1)
    sums = jnp.sum(DR[...].astype(F32), axis=0)
    recon = rc16[...].astype(F32)
    back = cpad[tp].astype(F32) + sums[1] + recon - apad[tp].astype(F32)
    ZB[0] = back.astype(BF)
    if stop == 11:
        return finish()

    gy = Gather(ZB, Y, 1)
    gy.start()
    out_ref[...] = (recon + sums[0]).astype(BF)[:, :W]
    gy.forward(0)
    if stop == 12:
        return finish()
    gy.forward(1)
    if stop == 13:
        return finish()

    acc[...] = jnp.zeros_like(acc)

    def back_part(h, lo, hi):
        s = acc[h]
        for i in range(lo, hi):
            lhs = jnp.concatenate([Y[h, :, 0, i].reshape(128, 128), Y[h, :, 1, i].reshape(128, 128)], axis=1)
            s = s + mm(lhs, WDT[i].reshape(256, 128))
        acc[h] = s

    got("t0")
    gy.swap(0)
    back_part(c, 0, NEAR)
    got("t1")
    gy.swap(1)
    back_part(c, NEAR, NZ)
    got("sis10")
    back_part(oc, 0, NEAR)
    got("sis11")
    back_part(oc, NEAR, NZ)
    if stop == 14:
        return finish()
    bact = (acc[...].reshape(256, 128) * hit[...]).astype(BF)
    gencb_ref[...] = jnp.sum(bact.astype(F32), axis=0)
    gdecb_ref[...] = jnp.sum(Y[:, :, c, 0].reshape(256, 128).astype(F32), axis=0)[:W]
    actf[...] = bact.reshape(2, 128, 128)

    def enc_grad(k):
        h = k // NZ
        s = lax.rem(k, NZ)
        rows = pl.ds(pl.multiple_of((2 * z_at(s) + h) * W, 16), W)
        genc_ref[rows, :] = mm(XT[h, s], actf[...].reshape(256, 128))[:W].astype(BF)

    lax.fori_loop(0, 2 * NZ, lambda k, n: (enc_grad(k), n)[1], 0, unroll=4)
    for i in range(2 * NZ):
        y = Y[:, :, i % 2, slot_of(i // 2 - z)].reshape(256, 128)
        gdec_ref[:, i * W:(i + 1) * W] = mm(actt[...], y)[:, :W].astype(BF)
    finish()


def step(activations, indices, w_enc, b_enc, w_dec, b_dec, w_gate, w_up, w_down, cotangent, stop=99, cid=1):
    vm = pltpu.VMEM
    dma = pltpu.SemaphoreType.DMA
    inside = pl.BlockSpec(memory_space=pltpu.VMEM)
    outside = pl.BlockSpec(memory_space=pl.ANY)
    return pl.pallas_call(
        functools.partial(kernel, stop),
        out_shape=(
            jax.ShapeDtypeStruct((16, W), BF),
            jax.ShapeDtypeStruct((2 * NZ * W, 128), BF),
            jax.ShapeDtypeStruct((128,), F32),
            jax.ShapeDtypeStruct((128, 2 * NZ * W), BF),
            jax.ShapeDtypeStruct((W,), F32),
        ),
        in_specs=[inside, inside, outside, inside, outside, inside, outside, outside, outside, inside],
        out_specs=[inside] * 5,
        scratch_shapes=[
            vm((NT, 16, 128), BF),
            vm((NT, 16, 128), BF),
            vm((NZ, 16, 128), BF),
            vm((NZ, 16, 128), BF),
            vm((2, 8, 2, NZ, 16, 128), BF),
            vm((2, 8, 2, NZ, 16, 128), BF),
            vm((2, NZ, 128, 256), BF),
            vm((2, NZ, 2, 128, 128), BF),
            vm((2, 2, NZ, 128, 128), BF),
            vm((NZ, 2, 128, 128), BF),
            vm((256, 128), F32),
            vm((2, 128, 128), F32),
            vm((2, 8, 128), F32),
            vm((128, 256), BF),
            vm((2, 128, 128), BF),
            vm((128, 256), BF),
            vm((2, 128, 128), F32),
            vm((8, 2, NZ, 16, 128), BF),
            vm((NT, NZ, 16, 128), BF),
            vm((NZ, 16, 128), BF),
            vm((NZ, 16, 128), BF),
            vm((16, 128), BF),
            vm((MEM, TB, 16, 128), BF),
            vm((MEM, 128, FF), BF),
            vm((MEM, 128, FF), BF),
            vm((MEM, FF, 128), BF),
            vm((MEM, FF, 128), BF),
            vm((MEM, FF, 128), BF),
            vm((MEM, TB, 16, 128), BF),
            vm((NP, 8, FF), F32),
            vm((NP, 8, FF), F32),
            vm((NP, 8, FF), F32),
            vm((NP, 16, FF), BF),
            vm((NP, 16, FF), BF),
            vm((NP, 16, FF), BF),
            vm((MEM, TB, 2, 16, 128), BF),
            vm((NT, 2, 16, 128), BF),
            vm((NP, 8, FF), F32),
            vm((NP, 8, FF), F32),
            vm((NP, 8, FF), F32),
            vm((128, 2 * NZ * W), BF),
            vm((128, FF), BF),
            dma((9,)), dma((9,)),
            dma((7, NZ)), dma((7, NZ)),
            dma((8, NT)), dma((8, NT)),
            dma((4, MEM, 2)), dma((4, MEM)),
            dma((4 + 2 * NZ,)),
        ],
        compiler_params=pltpu.CompilerParams(
            collective_id=cid, has_side_effects=True, vmem_limit_bytes=56 * 2**20
        ),
        cost_estimate=pl.CostEstimate(flops=2 * 10**9, bytes_accessed=6 * 10**6, transcendentals=10**5),
        name="sae_step",
    )(
        activations.T, indices.T, w_enc, b_enc.reshape(1, 128), w_dec, b_dec.reshape(1, W),
        w_gate, w_up, w_down.T, cotangent.T,
    )


def solution(mesh):
    return jax.shard_map(
        step,
        mesh=mesh,
        in_specs=(
            P(None, "lat"),
            P(),
            P(None, ("lat", "tp")),
            P(("lat", "tp")),
            P(("lat", "tp"), None),
            P("lat"),
            P("lat", "tp"),
            P("lat", "tp"),
            P("tp", "lat"),
            P(None, "lat"),
        ),
        out_specs=(
            P("tp", "lat"),
            P(None, ("lat", "tp")),
            P(("lat", "tp")),
            P(("lat", "tp"), None),
            P("lat"),
        ),
        check_vma=False,
    )
```

```python
import functools

import jax
import jax.numpy as jnp
from jax import lax
from jax.experimental import pallas as pl
from jax.experimental.pallas import tpu as pltpu
from jax.sharding import PartitionSpec as P

MESH = pl.DeviceIdType.MESH
NZ = 16
NT = 16
PAIR = 2
MEM = 2 * PAIR
NP = NZ // PAIR
TB = NT // MEM
RB = 16 * TB
W = 112
FF = 896
NEAR = 9
BF = jnp.bfloat16
F32 = jnp.float32


def mm(a, b):
    return lax.dot_general(a, b, (((1,), (0,)), ((), ())), preferred_element_type=F32)


def mm_nt(a, b):
    return lax.dot_general(a, b, (((1,), (1,)), ((), ())), preferred_element_type=F32)


def gelu_parts(value):
    coeff = 0.7978845608028654
    inner = coeff * (value + 0.044715 * value * value * value)
    tanh_term = jnp.tanh(inner)
    gelu_value = 0.5 * value * (1.0 + tanh_term)
    slope = 0.5 * (1.0 + tanh_term) + 0.5 * value * (1.0 - tanh_term * tanh_term) * coeff * (
        1.0 + 3.0 * 0.044715 * value * value
    )
    return gelu_value, slope


def offset(s):
    return (s + 1) // 2 * (2 * (s % 2) - 1)


def mirror(s):
    return s if s in (0, NZ - 1) else s + 2 * (s % 2) - 1


def plus(v, d, n):
    v = v + d
    return v if d == 0 else jnp.where(v >= n, v - n, v) if d > 0 else jnp.where(v < 0, v + n, v)


def slot_of(d):
    d = lax.rem(d + NZ, NZ)
    return jnp.maximum(jnp.where(d <= NZ // 2, 2 * d - 1, 2 * (NZ - d)), 0)


def folded(v):
    rest = jnp.concatenate([v[..., 512:], jnp.zeros(v.shape[:-1] + (128,), v.dtype)], axis=-1)
    return jnp.concatenate([v[..., :512], rest], axis=-2)


def unfolded(v):
    return jnp.concatenate([v[..., :8, :], v[..., 8:, :384]], axis=-1)


def loop(n, body, start=0):
    for k in range(start, n):
        body(k)


def kernel(
    stop,
    at_ref, idxt_ref, wenc_ref, benc_ref, wdec_ref, bdec_ref, wg_ref, wu_ref, wnt_ref, cott_ref,
    out_ref, genc_ref, gencb_ref, gdec_ref, gdecb_ref,
    apad, cpad, ZA, ZB, X, Y, XT, WE, WD, WDT, hit, hit2, bias2, act, actf, actt, acc, S2, R2, S3, R3, rc16, RC,
    WG, WU, WGT, WUT, WN, CT, BS, BR, BG, CS, CR, AG, DS, DR, DT, RT, HID, BGT, BUP, wdec, wnt,
    s_s, s_r, z_s, z_r, t_s, t_r, g_s, g_r, l_s,
):
    lat = lax.axis_index("lat")
    tp = lax.axis_index("tp")
    z = lat // 2
    c = lax.rem(lat, 2)
    p = lat // MEM
    m = lax.rem(lat, MEM)
    oc = 1 - c
    ht = tp // 8
    jt = lax.rem(tp, 8)
    mt = tp // TB
    slot = lax.rem(tp, TB)
    sister = lat + 1 - 2 * c
    partner = MEM * p + lax.rem(m + 2, MEM)
    drains = []
    comes = {}

    def finish():
        for wait in comes.values():
            wait()
        for wait in drains:
            wait()

    def got(name):
        comes.pop(name)()

    def copy(src, dst, ss, rs, dl, dt):
        return pltpu.make_async_remote_copy(
            src_ref=src, dst_ref=dst, send_sem=ss, recv_sem=rs, device_id=(dl, dt), device_id_type=MESH
        )

    def to_sister(src, dst, n):
        return copy(src, dst, s_s.at[n], s_r.at[n], sister, tp)

    def z_at(s):
        return plus(z, offset(s), NZ)

    bar = pltpu.get_barrier_semaphore()

    def hello_z(k):
        pl.semaphore_signal(bar, inc=1, device_id=(2 * z_at(NZ - 1 - k) + c, tp), device_id_type=MESH)

    def hello_t(k):
        kk = k + 1
        mo = plus(m, kk // NT, MEM)
        to = plus(tp, kk % NT, NT)
        pl.semaphore_signal(bar, inc=1, device_id=(MEM * p + mo, to), device_id_type=MESH)

    loop(NZ - 1, hello_z)
    loop(MEM * NT - 1, hello_t)

    top = pl.ds(0, W)
    l_wnt = pltpu.make_async_copy(wnt_ref, wnt.at[top], l_s.at[0])
    l_wg = pltpu.make_async_copy(wg_ref, WG.at[m, top], l_s.at[1])
    l_wu = pltpu.make_async_copy(wu_ref, WU.at[m, top], l_s.at[2])
    l_wd = pltpu.make_async_copy(wdec_ref, wdec, l_s.at[3])

    def l_we(k):
        h = k // NZ
        s = k % NZ
        rows = pl.ds(pl.multiple_of((2 * z_at(s) + h) * W, 16), W)
        return pltpu.make_async_copy(wenc_ref.at[rows], WE.at[c, s, h, top], l_s.at[4 + k])

    l_wnt.start()
    loop(2 * NZ, lambda k: l_we(k).start())
    l_wd.start()
    l_wg.start()
    l_wu.start()

    fill = jnp.zeros((128 - W, 256), BF)
    apad[...] = jnp.concatenate([at_ref[...], fill], axis=0).T.reshape(NT, 16, 128)
    cpad[...] = jnp.concatenate([cott_ref[...], fill], axis=0).T.reshape(NT, 16, 128)
    ZA[0] = apad[tp]

    def pad_w(g):
        WG[g, W:] = jnp.zeros((128 - W, FF), BF)
        WU[g, W:] = jnp.zeros((128 - W, FF), BF)

    def pad_e(k):
        WE[c, k // 2, k % 2, W:] = jnp.zeros((128 - W, 128), BF)

    loop(MEM, pad_w)
    loop(2 * NZ, pad_e)
    wnt[W:] = jnp.zeros((128 - W, FF), BF)
    CT[m] = cpad[pl.ds(m * TB, TB)]
    l_wnt.wait()
    WN[m] = wnt[...].T

    pl.semaphore_wait(bar, NZ - 1 + MEM * NT - 1)
    if stop == 0:
        loop(2 * NZ, lambda k: l_we(k).wait())
        l_wg.wait()
        l_wu.wait()
        l_wd.wait()
        return finish()

    class Gather:
        def __init__(self, zb, buf, n):
            self.zb, self.buf, self.n = zb, buf, n

        def z_out(self, s):
            r = mirror(s)
            return copy(self.zb.at[0], self.zb.at[r], z_s.at[self.n, s], z_r.at[self.n, r], 2 * z_at(s) + c, tp)

        def z_in(self, s):
            return copy(self.zb.at[s], self.zb.at[s], z_s.at[self.n, s], z_r.at[self.n, s], 2 * z_at(s) + c, tp)

        def rows(self, w):
            return pl.ds(0, NEAR) if w == 0 else pl.ds(NEAR, NZ - NEAR)

        def t_out(self, w, d):
            to = plus(tp, d, NT)
            sem = 2 * self.n + w
            return copy(self.zb.at[self.rows(w)], self.buf.at[ht, jt, c, self.rows(w)],
                        t_s.at[sem, to], t_r.at[sem, c * 8 + jt], 2 * z + ht, to)

        def t_in(self, w, k):
            e = plus(c, k // 8, 2)
            j = plus(jt, k % 8, 8)
            dst = self.buf.at[c, j, e, self.rows(w)]
            sem = 2 * self.n + w
            return copy(dst, dst, t_s.at[sem, 0], t_r.at[sem, e * 8 + j], 2 * z + e, c * 8 + j)

        def sis(self, which, w):
            part = self.buf.at[which, :, :, self.rows(w)]
            return to_sister(part, part, 2 * self.n + w)

        def start(self):
            loop(NZ - 1, lambda k: self.z_out(NZ - 1 - k).start())
            drains.append(lambda: loop(NZ, lambda s: self.z_out(s).wait_send(), 1))
            comes["z0"] = lambda: loop(NEAR, lambda s: self.z_in(s).wait_recv(), 1)
            comes["z1"] = lambda: loop(NZ, lambda s: self.z_in(s).wait_recv(), NEAR)

        def forward(self, w):
            got("z%d" % w)
            loop(NT, lambda d: self.t_out(w, d).start(), 1)

            @pl.when(ht != c)
            def _():
                self.t_out(w, 0).start()

            @pl.when(ht == c)
            def _():
                self.buf[c, jt, c, self.rows(w)] = self.zb[self.rows(w)]

            def drain():
                loop(NT, lambda d: self.t_out(w, d).wait_send(), 1)

                @pl.when(ht != c)
                def _():
                    self.t_out(w, 0).wait_send()

            def come():
                loop(NT, lambda k: self.t_in(w, k).wait_recv(), 1)

                @pl.when(ht != c)
                def _():
                    self.t_in(w, 0).wait_recv()

            drains.append(drain)
            comes["t%d" % w] = come

        def swap(self, w):
            self.sis(c, w).start()
            drains.append(lambda: self.sis(c, w).wait_send())
            comes["sis%d%d" % (self.n, w)] = lambda: self.sis(oc, w).wait_recv()

    ga = Gather(ZA, X, 0)
    ga.start()

    def weight(a, i):
        return [WN.at[i], WG.at[i, top], WU.at[i, top]][a]

    def share(a, i, to):
        return copy(weight(a, i), weight(a, i), g_s.at[a, i, 0 if to is sister else 1], g_r.at[a, i], to, tp)

    slot_p = lax.rem(m + 2, MEM)
    slot_s = m + 1 - 2 * c
    slot_sp = lax.rem(slot_s + 2, MEM)

    def share_out(a):
        share(a, m, sister).start()
        share(a, m, partner).start()
        drains.append(lambda: [share(a, m, sister).wait_send(), share(a, m, partner).wait_send()])
        comes["sis w%d" % a] = lambda: share(a, slot_s, sister).wait_recv()
        comes["chip w%d" % a] = lambda: share(a, slot_p, partner).wait_recv()

    def share_on(a):
        got("chip w%d" % a)
        share(a, slot_p, sister).start()
        drains.append(lambda: share(a, slot_p, sister).wait_send())
        comes["last w%d" % a] = lambda: share(a, slot_sp, sister).wait_recv()

    def cot_out(d):
        mo = plus(m, d, MEM)
        return copy(cpad.at[pl.ds(mo * TB, TB)], CT.at[m], g_s.at[3, mo, 0], g_r.at[3, m], MEM * p + mo, tp)

    def cot_in(d):
        mo = plus(m, d, MEM)
        return copy(CT.at[mo], CT.at[mo], g_s.at[3, mo, 0], g_r.at[3, mo], MEM * p + mo, tp)

    loop(MEM, lambda d: cot_out(d).start(), 1)
    drains.append(lambda: loop(MEM, lambda d: cot_out(d).wait_send(), 1))
    comes["cot"] = lambda: loop(MEM, lambda d: cot_in(d).wait_recv(), 1)
    share_out(0)

    ids_col = (lat * NT + tp) * 128 + lax.broadcasted_iota(jnp.int32, (128, 256), 0)

    def one_hit(j, found):
        return jnp.where(idxt_ref[pl.ds(j, 1), :] == ids_col, 1.0, found)

    hit[...] = lax.fori_loop(0, idxt_ref.shape[0], one_hit, jnp.zeros((128, 256), F32), unroll=8).T
    other_rows = pl.ds(pl.multiple_of(oc * 128, 128), 128)
    own_rows = pl.ds(pl.multiple_of(c * 128, 128), 128)
    hit2[c] = hit[own_rows, :]

    def hit_swap():
        return to_sister(hit.at[other_rows], hit2.at[c], 4)

    hit_swap().start()
    drains.append(lambda: hit_swap().wait_send())
    bias2[c] = jnp.broadcast_to(benc_ref[...], (8, 128))

    def bias_swap(i):
        return to_sister(bias2.at[i], bias2.at[i], 8)

    bias_swap(c).start()
    drains.append(lambda: bias_swap(c).wait_send())
    comes["bias"] = lambda: bias_swap(oc).wait_recv()
    comes["hit"] = lambda: to_sister(hit2.at[oc], hit2.at[oc], 4).wait_recv()

    loop(2 * NZ, lambda k: l_we(k).wait())

    def enc_swap(i):
        return to_sister(WE.at[i], WE.at[i], 5)

    enc_swap(c).start()
    drains.append(lambda: enc_swap(c).wait_send())
    comes["enc"] = lambda: enc_swap(oc).wait_recv()

    ga.forward(0)

    l_wd.wait()

    def dec_block(i):
        blk = jnp.concatenate([wdec[:, i * W:(i + 1) * W], jnp.zeros((128, 128 - W), BF)], axis=1)
        s = slot_of(i // 2 - z)
        WD[c, i % 2, s] = blk
        WDT[s, i % 2] = blk.T

    for i in range(NZ):
        dec_block(i)
    ga.forward(1)
    for i in range(NZ, 2 * NZ):
        dec_block(i)

    def dec_swap(i):
        return to_sister(WD.at[i], WD.at[i], 6)

    dec_swap(c).start()
    drains.append(lambda: dec_swap(c).wait_send())
    comes["dec"] = lambda: dec_swap(oc).wait_recv()
    share_on(0)
    if stop == 1:
        return finish()

    def ring(src, dst, n, own_src, send, d):
        q = plus(p, d, NP)
        if send:
            return copy(src.at[q] if own_src else src, dst.at[p], z_s.at[n, q], z_r.at[n, p], MEM * q + m, tp)
        return copy(dst.at[q], dst.at[q], z_s.at[n, q], z_r.at[n, q], MEM * q + m, tp)

    def far(k):
        return NP // 2 + (k + 1) // 2 * (1 - 2 * (k % 2))

    def ring_start(src, dst, n, own_src, name):
        loop(NP - 1, lambda k: ring(src, dst, n, own_src, True, far(k)).start())
        drains.append(lambda: loop(NP, lambda d: ring(src, dst, n, own_src, True, d).wait_send(), 1))
        comes[name] = lambda: loop(NP, lambda d: ring(src, dst, n, own_src, False, d).wait_recv(), 1)

    got("cot")
    got("sis w0")
    got("last w0")
    bh = mm_nt(CT[0].reshape(RB, 128), WN[0])
    for g in range(1, MEM):
        bh = bh + mm_nt(CT[g].reshape(RB, 128), WN[g])
    BS[...] = folded(bh.reshape(NP, 8, FF)).astype(BF)
    BR[p] = BS[p]
    ring_start(BS, BR, 2, True, "bh sum")
    l_wg.wait()
    l_wu.wait()
    share_out(1)
    share_out(2)
    if stop == 2:
        return finish()

    def pre_part(start, lo, hi):
        pre = start
        for i in range(lo, hi):
            lhs = jnp.concatenate([X[c, :, 0, i].reshape(128, 128), X[c, :, 1, i].reshape(128, 128)], axis=1)
            rhs = jnp.concatenate([WE[0, i].reshape(256, 128), WE[1, i].reshape(256, 128)], axis=1)
            pre = pre + mm(lhs, rhs)
        return pre

    got("bias")
    got("enc")
    got("hit")
    got("t0")
    ga.swap(0)
    pre = pre_part(jnp.concatenate([bias2[0, 0:1], bias2[1, 0:1]], axis=1), 0, NEAR)
    got("t1")
    ga.swap(1)
    pre = pre_part(pre, NEAR, NZ)
    act[...] = (pre * jnp.concatenate([hit2[0], hit2[1]], axis=1)).astype(BF)
    if stop == 3:
        return finish()

    got("dec")
    half = NZ // 2

    def tsum_out(w, k):
        rows = pl.ds(w * half, half)
        e = plus(c, k // 8, 2)
        j = plus(jt, k % 8, 8)
        return copy(S2.at[j, e, rows], R2.at[tp, rows], t_s.at[4 + w, k], t_r.at[4 + w, tp], 2 * z + e,
                    c * 8 + j)

    def tsum_in(w, o):
        rows = pl.ds(w * half, half)
        return copy(R2.at[o, rows], R2.at[o, rows], t_s.at[4 + w, o], t_r.at[4 + w, o], 2 * z + ht, o)

    def tsum_drain(w):
        loop(NT, lambda k: tsum_out(w, k).wait_send(), 1)

        @pl.when(ht != c)
        def _():
            tsum_out(w, 0).wait_send()

    def tsum_come(w):
        loop(NT, lambda d: tsum_in(w, plus(tp, d, NT)).wait_recv(), 1)

        @pl.when(ht != c)
        def _():
            tsum_in(w, tp).wait_recv()

    for w in (1, 0):
        for i in range(w * half, (w + 1) * half):
            rhs = jnp.concatenate([jnp.concatenate([WD[0, e, i], WD[1, e, i]], axis=0) for e in (0, 1)], axis=1)
            both = mm(act[...], rhs).astype(BF)
            S2[:, 0, i] = both[:, :128].reshape(8, 16, 128)
            S2[:, 1, i] = both[:, 128:].reshape(8, 16, 128)
        loop(NT, lambda k: tsum_out(w, k).start(), 1)

        @pl.when(ht != c)
        def _():
            tsum_out(w, 0).start()

        @pl.when(ht == c)
        def _():
            rows = pl.ds(w * half, half)
            R2[tp, rows] = S2[jt, c, rows]

        drains.append(functools.partial(tsum_drain, w))
        comes["ts%d" % w] = functools.partial(tsum_come, w)
    if stop == 4:
        return finish()

    actf[c] = act[:, pl.ds(pl.multiple_of(c * 128, 128), 128)]

    def act_swap():
        return to_sister(act.at[:, pl.ds(pl.multiple_of(oc * 128, 128), 128)], actf.at[c], 7)

    act_swap().start()
    drains.append(lambda: act_swap().wait_send())
    comes["act"] = lambda: to_sister(actf.at[oc], actf.at[oc], 7).wait_recv()

    got("bh sum")
    BG[p] = jnp.sum(BR[...].astype(F32), axis=0).astype(BF)
    ring_start(BG.at[p], BG, 3, False, "bh")
    share_on(1)
    share_on(2)
    got("sis00")
    got("sis01")
    def z_out(s):
        r = mirror(s)
        return copy(S3.at[s], R3.at[r], z_s.at[4, s], z_r.at[4, r], 2 * z_at(s) + c, tp)

    def z_in(s):
        return copy(R3.at[s], R3.at[s], z_s.at[4, s], z_r.at[4, s], 2 * z_at(s) + c, tp)

    def tadd(s):
        S3[s] = jnp.sum(R2[:, s].astype(F32), axis=0).astype(BF)

    def far_sum(k):
        tadd(NZ - 1 - k)
        z_out(NZ - 1 - k).start()

    got("ts1")
    loop(half, far_sum)
    got("ts0")
    loop(half - 1, lambda k: far_sum(k + half))
    tadd(0)
    R3[0] = S3[0]
    drains.append(lambda: loop(NZ, lambda s: z_out(s).wait_send(), 1))
    comes["z sum"] = lambda: loop(NZ, lambda s: z_in(s).wait_recv(), 1)
    if stop == 5:
        return finish()
    for a in (1, 2):
        got("sis w%d" % a)
        got("last w%d" % a)
    for g in range(MEM // 2):
        WGT[g] = WG[2 * g:2 * g + 2].reshape(256, FF).T
        WUT[g] = WU[2 * g:2 * g + 2].reshape(256, FF).T
    got("z sum")
    bias = jnp.concatenate([bdec_ref[...], jnp.zeros((1, 128 - W), F32)], axis=1)
    rc16[...] = (jnp.sum(R3[...].astype(F32), axis=0) + bias).astype(BF)
    if stop == 6:
        return finish()

    def rcopy(d):
        o = plus(tp, d, NT)
        return copy(rc16, RC.at[m, slot], t_s.at[6, o], t_r.at[6, m * TB + slot], MEM * p + mt, o)

    def member(k):
        return plus(m, k // TB, MEM), plus(slot, k % TB, TB)

    def rwait(k):
        g, i = member(k)
        copy(rc16, RC.at[g, i], t_s.at[6, 0], t_r.at[6, g * TB + i], MEM * p + g, m * TB + i).wait_recv()

    loop(NT, lambda d: rcopy(d).start(), 1)

    @pl.when(mt == m)
    def _():
        RC[m, slot] = rc16[...]

    @pl.when(mt != m)
    def _():
        rcopy(0).start()

    def rdrain():
        loop(NT, lambda d: rcopy(d).wait_send(), 1)

        @pl.when(mt != m)
        def _():
            rcopy(0).wait_send()

    drains.append(rdrain)
    loop(MEM * TB, rwait, 1)

    @pl.when(mt != m)
    def _():
        rwait(0)

    if stop == 7:
        return finish()

    def pairs(i):
        return jnp.concatenate([RC[2 * i].reshape(RB, 128), RC[2 * i + 1].reshape(RB, 128)], axis=1)

    gate = mm(pairs(0), WG[0:2].reshape(256, FF))
    up = mm(pairs(0), WU[0:2].reshape(256, FF))
    for i in range(1, MEM // 2):
        gate = gate + mm(pairs(i), WG[2 * i:2 * i + 2].reshape(256, FF))
        up = up + mm(pairs(i), WU[2 * i:2 * i + 2].reshape(256, FF))
    CS[...] = jnp.concatenate([gate.reshape(NP, 8, FF), up.reshape(NP, 8, FF)], axis=1).astype(BF)
    ring_start(CS, CR, 5, True, "gate sum")
    CR[p] = CS[p]
    for h in range(2):
        for i in range(NZ):
            XT[h, i] = X[:, :, h, i].reshape(256, 128).T
    got("act")
    actt[...] = actf[...].reshape(256, 128).T
    if stop == 8:
        return finish()
    got("gate sum")
    AG[p] = jnp.sum(CR[...].astype(F32), axis=0).astype(BF)
    ring_start(AG.at[p], AG, 6, False, "gate")
    got("bh")
    got("gate")
    if stop == 9:
        return finish()

    def cells(i):
        both_ = AG[i].astype(F32)
        gate_, up_ = both_[:8], both_[8:]
        bh_ = unfolded(BG[i].astype(F32))
        gelu_value, slope = gelu_parts(gate_)
        HID[i] = gelu_value * up_
        BGT[i] = bh_ * up_ * slope
        BUP[i] = bh_ * gelu_value

    loop(NP, cells)
    bgate = BGT[...].reshape(RB, FF).astype(BF)
    bup = BUP[...].reshape(RB, FF).astype(BF)
    for g in range(MEM // 2):
        both = (mm(bgate, WGT[g]) + mm(bup, WUT[g])).astype(BF)
        DT[2 * g] = both[:, :128].reshape(TB, 16, 128)
        DT[2 * g + 1] = both[:, 128:].reshape(TB, 16, 128)
    if stop == 10:
        return finish()

    class Sums:
        def __init__(self, src, dst, n):
            self.src, self.dst, self.n = src, dst, n

        def out(self, k):
            g, i = member(k)
            return copy(self.src.at[g, i], self.dst.at[tp], t_s.at[self.n, k], t_r.at[self.n, tp], MEM * p + g,
                        m * TB + i)

        def come(self, d):
            o = plus(tp, d, NT)
            return copy(self.dst.at[o], self.dst.at[o], t_s.at[self.n, 0], t_r.at[self.n, o], MEM * p + mt, o)

        def start(self, name):
            loop(MEM * TB, lambda k: self.out(k).start(), 1)

            @pl.when(mt != m)
            def _():
                self.out(0).start()

            @pl.when(mt == m)
            def _():
                self.dst[tp] = self.src[m, slot]

            def drain():
                loop(MEM * TB, lambda k: self.out(k).wait_send(), 1)

                @pl.when(mt != m)
                def _():
                    self.out(0).wait_send()

            def wait():
                loop(NT, lambda d: self.come(d).wait_recv(), 1)

                @pl.when(mt != m)
                def _():
                    self.come(0).wait_recv()

            drains.append(drain)
            comes[name] = wait

    Sums(DT, RT, 7).start("through")
    hidden = HID[...].reshape(RB, FF).astype(BF)
    for g in range(MEM // 2):
        both = mm(hidden, jnp.concatenate([WN[2 * g], WN[2 * g + 1]], axis=1)).astype(BF)
        DS[2 * g] = both[:, :128].reshape(TB, 16, 128)
        DS[2 * g + 1] = both[:, 128:].reshape(TB, 16, 128)
    base = cpad[tp].astype(F32) + rc16[...].astype(F32) - apad[tp].astype(F32)
    got("through")
    ZB[0] = (base + jnp.sum(RT[...].astype(F32), axis=0)).astype(BF)
    if stop == 11:
        return finish()

    gy = Gather(ZB, Y, 1)
    gy.start()
    gy.forward(0)
    if stop == 12:
        return finish()
    gy.forward(1)
    Sums(DS, DR, 8).start("down")
    if stop == 13:
        return finish()

    acc[...] = jnp.zeros_like(acc)

    def back_part(h, lo, hi):
        s = acc[h]
        for i in range(lo, hi):
            lhs = jnp.concatenate([Y[h, :, 0, i].reshape(128, 128), Y[h, :, 1, i].reshape(128, 128)], axis=1)
            s = s + mm(lhs, WDT[i].reshape(256, 128))
        acc[h] = s

    def dec_part(lo, hi):
        for i in range(lo, hi):
            rhs = jnp.concatenate([Y[:, :, h, i].reshape(256, 128) for h in range(2)], axis=1)
            both = mm(actt[...], rhs).astype(BF)
            gdec_ref[2 * z_at(i)] = both[:, :128]
            gdec_ref[2 * z_at(i) + 1] = both[:, 128:]

    got("t0")
    gy.swap(0)
    back_part(c, 0, NEAR)
    got("t1")
    gy.swap(1)
    back_part(c, NEAR, NZ)
    got("sis10")
    back_part(oc, 0, NEAR)
    dec_part(0, NEAR)
    got("down")
    out_ref[...] = (rc16[...].astype(F32) + jnp.sum(DR[...].astype(F32), axis=0)).astype(BF)[:, :W]
    got("sis11")
    back_part(oc, NEAR, NZ)
    if stop == 14:
        return finish()
    bact = (acc[...].reshape(256, 128) * hit[...]).astype(BF)
    gencb_ref[...] = jnp.sum(bact.astype(F32), axis=0)
    gdecb_ref[...] = jnp.sum(Y[:, :, c, 0].reshape(256, 128).astype(F32), axis=0)[:W]
    actf[...] = bact.reshape(2, 128, 128)

    def enc_grad(k):
        h = k // NZ
        s = k % NZ
        rows = pl.ds(pl.multiple_of((2 * z_at(s) + h) * W, 16), W)
        genc_ref[rows, :] = mm(XT[h, s], actf[...].reshape(256, 128))[:W].astype(BF)

    loop(2 * NZ, enc_grad)
    dec_part(NEAR, NZ)
    finish()


def hand_on(out_in, genc_in, gencb_in, gdec_in, gdecb_in, out_ref, genc_ref, gencb_ref, gdec_ref, gdecb_ref):
    out_ref[...] = out_in[...]
    genc_ref[...] = genc_in[...]
    gencb_ref[...] = gencb_in[...]
    gdecb_ref[...] = gdecb_in[...]
    for i in range(2 * NZ):
        gdec_ref[:, i * W:(i + 1) * W] = gdec_in[i][:, :W]


def step(activations, indices, w_enc, b_enc, w_dec, b_dec, w_gate, w_up, w_down, cotangent, stop=99, cid=1):
    vm = pltpu.VMEM
    dma = pltpu.SemaphoreType.DMA
    inside = pl.BlockSpec(memory_space=pltpu.VMEM)
    outside = pl.BlockSpec(memory_space=pl.ANY)
    shapes = (
        jax.ShapeDtypeStruct((16, W), BF),
        jax.ShapeDtypeStruct((2 * NZ * W, 128), BF),
        jax.ShapeDtypeStruct((128,), F32),
        jax.ShapeDtypeStruct((128, 2 * NZ * W), BF),
        jax.ShapeDtypeStruct((W,), F32),
    )
    held = shapes[:3] + (jax.ShapeDtypeStruct((2 * NZ, 128, 128), BF),) + shapes[4:]
    results = pl.pallas_call(
        functools.partial(kernel, stop),
        out_shape=held,
        in_specs=[inside, inside, outside, inside, outside, inside, outside, outside, outside, inside],
        out_specs=[inside] * 5,
        scratch_shapes=[
            vm((NT, 16, 128), BF),
            vm((NT, 16, 128), BF),
            vm((NZ, 16, 128), BF),
            vm((NZ, 16, 128), BF),
            vm((2, 8, 2, NZ, 16, 128), BF),
            vm((2, 8, 2, NZ, 16, 128), BF),
            vm((2, NZ, 128, 256), BF),
            vm((2, NZ, 2, 128, 128), BF),
            vm((2, 2, NZ, 128, 128), BF),
            vm((NZ, 2, 128, 128), BF),
            vm((256, 128), F32),
            vm((2, 128, 128), F32),
            vm((2, 8, 128), F32),
            vm((128, 256), BF),
            vm((2, 128, 128), BF),
            vm((128, 256), BF),
            vm((2, 128, 128), F32),
            vm((8, 2, NZ, 16, 128), BF),
            vm((NT, NZ, 16, 128), BF),
            vm((NZ, 16, 128), BF),
            vm((NZ, 16, 128), BF),
            vm((16, 128), BF),
            vm((MEM, TB, 16, 128), BF),
            vm((MEM, 128, FF), BF),
            vm((MEM, 128, FF), BF),
            vm((MEM // 2, FF, 256), BF),
            vm((MEM // 2, FF, 256), BF),
            vm((MEM, FF, 128), BF),
            vm((MEM, TB, 16, 128), BF),
            vm((NP, 16, 512), BF),
            vm((NP, 16, 512), BF),
            vm((NP, 16, 512), BF),
            vm((NP, 16, FF), BF),
            vm((NP, 16, FF), BF),
            vm((NP, 16, FF), BF),
            vm((MEM, TB, 16, 128), BF),
            vm((NT, 16, 128), BF),
            vm((MEM, TB, 16, 128), BF),
            vm((NT, 16, 128), BF),
            vm((NP, 8, FF), F32),
            vm((NP, 8, FF), F32),
            vm((NP, 8, FF), F32),
            vm((128, 2 * NZ * W), BF),
            vm((128, FF), BF),
            dma((9,)), dma((9,)),
            dma((7, NZ)), dma((7, NZ)),
            dma((9, NT)), dma((9, NT)),
            dma((4, MEM, 2)), dma((4, MEM)),
            dma((4 + 2 * NZ,)),
        ],
        compiler_params=pltpu.CompilerParams(
            collective_id=cid, has_side_effects=True, vmem_limit_bytes=56 * 2**20
        ),
        cost_estimate=pl.CostEstimate(flops=2 * 10**9, bytes_accessed=6 * 10**6, transcendentals=10**5),
        name="sae_step",
    )(
        activations.T, indices.T, w_enc, b_enc.reshape(1, 128), w_dec, b_dec.reshape(1, W),
        w_gate, w_up, w_down.T, cotangent.T,
    )
    return pl.pallas_call(
        hand_on,
        out_shape=shapes,
        in_specs=[inside] * 5,
        out_specs=[inside] * 5,
        compiler_params=pltpu.CompilerParams(vmem_limit_bytes=60 * 2**20),
        name="results",
    )(*results)


def solution(mesh):
    return jax.shard_map(
        step,
        mesh=mesh,
        in_specs=(
            P(None, "lat"),
            P(),
            P(None, ("lat", "tp")),
            P(("lat", "tp")),
            P(("lat", "tp"), None),
            P("lat"),
            P("lat", "tp"),
            P("lat", "tp"),
            P("tp", "lat"),
            P(None, "lat"),
        ),
        out_specs=(
            P("tp", "lat"),
            P(None, ("lat", "tp")),
            P(("lat", "tp")),
            P(("lat", "tp"), None),
            P("lat"),
        ),
        check_vma=False,
    )
```

```python
import functools

import jax
import jax.numpy as jnp
from jax import lax
from jax.experimental import pallas as pl
from jax.experimental.pallas import tpu as pltpu
from jax.sharding import PartitionSpec as P

MESH = pl.DeviceIdType.MESH
NZ = 16
NT = 16
PAIR = 2
MEM = 2 * PAIR
NP = NZ // PAIR
TB = NT // MEM
RB = 16 * TB
W = 112
FF = 896
PARTS = ((0, 8), (8, 8))
PAD = 128 - W
BF = jnp.bfloat16
F32 = jnp.float32


def mm(a, b):
    return lax.dot_general(a, b, (((1,), (0,)), ((), ())), preferred_element_type=F32)


def mm_nt(a, b):
    return lax.dot_general(a, b, (((1,), (1,)), ((), ())), preferred_element_type=F32)


def gelu_parts(value):
    coeff = 0.7978845608028654
    inner = coeff * (value + 0.044715 * value * value * value)
    tanh_term = jnp.tanh(inner)
    gelu_value = 0.5 * value * (1.0 + tanh_term)
    slope = 0.5 * (1.0 + tanh_term) + 0.5 * value * (1.0 - tanh_term * tanh_term) * coeff * (
        1.0 + 3.0 * 0.044715 * value * value
    )
    return gelu_value, slope


def offset(s):
    return (s + 1) // 2 * (2 * (s % 2) - 1)


def mirror(s):
    return s if s in (0, NZ - 1) else s + 2 * (s % 2) - 1


def plus(v, d, n):
    v = v + d
    return v if d == 0 else jnp.where(v >= n, v - n, v) if d > 0 else jnp.where(v < 0, v + n, v)


def slot_of(d):
    d = lax.rem(d + NZ, NZ)
    return jnp.maximum(jnp.where(d <= NZ // 2, 2 * d - 1, 2 * (NZ - d)), 0)


def carry(block, last, k):
    return jnp.concatenate([block[:, :W], last[:, k * PAD:(k + 1) * PAD]], axis=1)


def carried(blocks):
    rest = jnp.zeros((blocks[0].shape[0], PAD), blocks[0].dtype)
    return jnp.concatenate([b[:, W:] for b in blocks] + [rest], axis=1)


def folded(v):
    rest = jnp.concatenate([v[..., 512:], jnp.zeros(v.shape[:-1] + (128,), v.dtype)], axis=-1)
    return jnp.concatenate([v[..., :512], rest], axis=-2)


def unfolded(v):
    return jnp.concatenate([v[..., :8, :], v[..., 8:, :384]], axis=-1)


def loop(n, body, start=0):
    for k in range(start, n):
        body(k)


def kernel(
    at_in, idxt_in, wenc_ref, benc_in, wdec_ref, bdec_in, wg_ref, wu_ref, wnt_ref, cott_in,
    out_ref, genc_out, gencb_ref, gdec_out, gdecb_ref,
    at_ref, idxt_ref, benc_ref, bdec_ref, cott_ref, genc_ref, gdec_ref,
    apad, cpad, ZA, ZB, ZAP, ZBP, X, Y, XT, WE, WD, WDT, hit, hit2, bias2, act, actf, actt, acc, S2, R2, S3, R3, rc16, RC,
    WG, WU, WGT, WUT, WN, CT, BS, BR, BG, CS, CR, AG, DS, DR, DT, RT, HID, BGT, BUP, wdec, wnt,
    s_s, s_r, z_s, z_r, t_s, t_r, g_s, g_r, l_s, o_s,
):
    lat = lax.axis_index("lat")
    tp = lax.axis_index("tp")
    z = lat // 2
    c = lax.rem(lat, 2)
    p = lat // MEM
    m = lax.rem(lat, MEM)
    oc = 1 - c
    ht = tp // 8
    jt = lax.rem(tp, 8)
    mt = tp // TB
    slot = lax.rem(tp, TB)
    sister = lat + 1 - 2 * c
    partner = MEM * p + lax.rem(m + 2, MEM)
    drains = []
    comes = {}

    def finish():
        for wait in comes.values():
            wait()
        for wait in drains:
            wait()

    def got(name):
        comes.pop(name)()

    def copy(src, dst, ss, rs, dl, dt):
        return pltpu.make_async_remote_copy(
            src_ref=src, dst_ref=dst, send_sem=ss, recv_sem=rs, device_id=(dl, dt), device_id_type=MESH
        )

    def to_sister(src, dst, n):
        return copy(src, dst, s_s.at[n], s_r.at[n], sister, tp)

    def z_at(s):
        return plus(z, offset(s), NZ)

    bar = pltpu.get_barrier_semaphore()

    def hello_z(k):
        pl.semaphore_signal(bar, inc=1, device_id=(2 * z_at(NZ - 1 - k) + c, tp), device_id_type=MESH)

    def hello_t(k):
        kk = k + 1
        mo = plus(m, kk // NT, MEM)
        to = plus(tp, kk % NT, NT)
        pl.semaphore_signal(bar, inc=1, device_id=(MEM * p + mo, to), device_id_type=MESH)

    loop(NZ - 1, hello_z)
    loop(MEM * NT - 1, hello_t)

    top = pl.ds(0, W)
    l_wnt = pltpu.make_async_copy(wnt_ref, wnt.at[top], l_s.at[0])
    l_wg = pltpu.make_async_copy(wg_ref, WG.at[m, top], l_s.at[1])
    l_wu = pltpu.make_async_copy(wu_ref, WU.at[m, top], l_s.at[2])
    l_wd = pltpu.make_async_copy(wdec_ref, wdec, l_s.at[3])

    def l_we(k):
        h = k // NZ
        s = k % NZ
        rows = pl.ds(pl.multiple_of((2 * z_at(s) + h) * W, 16), W)
        return pltpu.make_async_copy(wenc_ref.at[rows], WE.at[c, s, h, top], l_s.at[4 + k])

    def l_small(k):
        pairs = ((at_in, at_ref), (cott_in, cott_ref), (idxt_in, idxt_ref), (benc_in, benc_ref), (bdec_in, bdec_ref))
        return pltpu.make_async_copy(pairs[k][0], pairs[k][1], o_s.at[k])

    loop(5, lambda k: l_small(k).start())
    l_wnt.start()
    l_wg.start()
    l_wu.start()
    l_wd.start()
    loop(2 * NZ, lambda k: l_we(k).start())
    loop(5, lambda k: l_small(k).wait())

    fill = jnp.zeros((128 - W, 256), BF)
    apad[...] = jnp.concatenate([at_ref[...], fill], axis=0).T.reshape(NT, 16, 128)
    cpad[...] = jnp.concatenate([cott_ref[...], fill], axis=0).T.reshape(NT, 16, 128)
    ZA[0] = apad[tp]

    def pad_w(g):
        WG[g, W:] = jnp.zeros((128 - W, FF), BF)
        WU[g, W:] = jnp.zeros((128 - W, FF), BF)

    def pad_e(k):
        WE[c, k // 2, k % 2, W:] = jnp.zeros((128 - W, 128), BF)

    loop(MEM, pad_w)
    loop(2 * NZ, pad_e)
    wnt[W:] = jnp.zeros((128 - W, FF), BF)
    CT[m] = cpad[pl.ds(m * TB, TB)]
    l_wnt.wait()
    WN[m] = wnt[...].T

    ids_col = (lat * NT + tp) * 128 + lax.broadcasted_iota(jnp.int32, (128, 256), 0)

    def one_hit(j, found):
        return jnp.where(idxt_ref[pl.ds(j, 1), :] == ids_col, 1.0, found)

    hit[...] = lax.fori_loop(0, idxt_ref.shape[0], one_hit, jnp.zeros((128, 256), F32), unroll=8).T
    other_rows = pl.ds(pl.multiple_of(oc * 128, 128), 128)
    own_rows = pl.ds(pl.multiple_of(c * 128, 128), 128)
    hit2[c] = hit[own_rows, :]

    pl.semaphore_wait(bar, NZ - 1 + MEM * NT - 1)

    class Gather:
        def __init__(self, zb, zp, buf, n):
            self.zb, self.zp, self.buf, self.n = zb, zp, buf, n

        def z_out(self, s):
            r = mirror(s)
            return copy(self.zb.at[0], self.zb.at[r], z_s.at[self.n, s], z_r.at[self.n, r], 2 * z_at(s) + c, tp)

        def z_in(self, s):
            return copy(self.zb.at[s], self.zb.at[s], z_s.at[self.n, s], z_r.at[self.n, s], 2 * z_at(s) + c, tp)

        def rows(self, w):
            return pl.ds(8 * w, 7)

        def t_out(self, w, d):
            to = plus(tp, d, NT)
            sem = 3 * self.n + w
            return copy(self.zp.at[self.rows(w)], self.buf.at[ht, jt, c, self.rows(w)],
                        t_s.at[sem, to], t_r.at[sem, c * 8 + jt], 2 * z + ht, to)

        def t_in(self, w, k):
            e = plus(c, k // 8, 2)
            j = plus(jt, k % 8, 8)
            dst = self.buf.at[c, j, e, self.rows(w)]
            sem = 3 * self.n + w
            return copy(dst, dst, t_s.at[sem, 0], t_r.at[sem, e * 8 + j], 2 * z + e, c * 8 + j)

        def sis(self, which, w):
            part = self.buf.at[which, :, :, self.rows(w)]
            return to_sister(part, part, 3 * self.n + w)

        def start(self):
            loop(NZ - 1, lambda k: self.z_out(NZ - 1 - k).start())
            drains.append(lambda: loop(NZ, lambda s: self.z_out(s).wait_send(), 1))
            for w, (lo, n) in enumerate(PARTS):
                comes["z%d" % w] = functools.partial(
                    loop, lo + n, lambda s: self.z_in(s).wait_recv(), max(lo, 1))

        def forward(self, w):
            got("z%d" % w)
            last = self.zb[8 * w + 7]
            for k in range(7):
                self.zp[8 * w + k] = carry(self.zb[8 * w + k], last, k)
            loop(NT, lambda d: self.t_out(w, d).start(), 1)

            @pl.when(ht != c)
            def _():
                self.t_out(w, 0).start()

            @pl.when(ht == c)
            def _():
                self.buf[c, jt, c, self.rows(w)] = self.zp[self.rows(w)]

            def drain():
                loop(NT, lambda d: self.t_out(w, d).wait_send(), 1)

                @pl.when(ht != c)
                def _():
                    self.t_out(w, 0).wait_send()

            def come():
                loop(NT, lambda k: self.t_in(w, k).wait_recv(), 1)

                @pl.when(ht != c)
                def _():
                    self.t_in(w, 0).wait_recv()

            drains.append(drain)
            comes["t%d" % w] = come

        def unpack(self, h, w):
            for e in range(2):
                blocks = [self.buf[h, :, e, 8 * w + k].reshape(128, 128) for k in range(7)]
                self.buf[h, :, e, 8 * w + 7] = carried(blocks).reshape(8, 16, 128)

        def swap(self, w):
            self.sis(c, w).start()
            drains.append(lambda: self.sis(c, w).wait_send())
            comes["sis%d%d" % (self.n, w)] = lambda: self.sis(oc, w).wait_recv()

    ga = Gather(ZA, ZAP, X, 0)
    ga.start()

    def weight(a, i):
        return [WN.at[i], WG.at[i, top], WU.at[i, top]][a]

    def share(a, i, to):
        return copy(weight(a, i), weight(a, i), g_s.at[a, i, 0 if to is sister else 1], g_r.at[a, i], to, tp)

    slot_p = lax.rem(m + 2, MEM)
    slot_s = m + 1 - 2 * c
    slot_sp = lax.rem(slot_s + 2, MEM)

    def share_out(a):
        share(a, m, sister).start()
        share(a, m, partner).start()
        drains.append(lambda: [share(a, m, sister).wait_send(), share(a, m, partner).wait_send()])
        comes["sis w%d" % a] = lambda: share(a, slot_s, sister).wait_recv()
        comes["chip w%d" % a] = lambda: share(a, slot_p, partner).wait_recv()

    def share_on(a):
        got("chip w%d" % a)
        share(a, slot_p, sister).start()
        drains.append(lambda: share(a, slot_p, sister).wait_send())
        comes["last w%d" % a] = lambda: share(a, slot_sp, sister).wait_recv()

    def cot_out(d):
        mo = plus(m, d, MEM)
        return copy(cpad.at[pl.ds(mo * TB, TB)], CT.at[m], g_s.at[3, mo, 0], g_r.at[3, m], MEM * p + mo, tp)

    def cot_in(d):
        mo = plus(m, d, MEM)
        return copy(CT.at[mo], CT.at[mo], g_s.at[3, mo, 0], g_r.at[3, mo], MEM * p + mo, tp)

    loop(MEM, lambda d: cot_out(d).start(), 1)
    drains.append(lambda: loop(MEM, lambda d: cot_out(d).wait_send(), 1))
    comes["cot"] = lambda: loop(MEM, lambda d: cot_in(d).wait_recv(), 1)
    share_out(0)

    def hit_swap():
        return to_sister(hit.at[other_rows], hit2.at[c], 6)

    hit_swap().start()
    drains.append(lambda: hit_swap().wait_send())
    bias2[c] = jnp.broadcast_to(benc_ref[...], (8, 128))

    def bias_swap(i):
        return to_sister(bias2.at[i], bias2.at[i], 10)

    bias_swap(c).start()
    drains.append(lambda: bias_swap(c).wait_send())
    comes["bias"] = lambda: bias_swap(oc).wait_recv()
    comes["hit"] = lambda: to_sister(hit2.at[oc], hit2.at[oc], 6).wait_recv()

    loop(2 * NZ, lambda k: l_we(k).wait())

    def enc_swap(i):
        return to_sister(WE.at[i], WE.at[i], 7)

    enc_swap(c).start()
    drains.append(lambda: enc_swap(c).wait_send())
    comes["enc"] = lambda: enc_swap(oc).wait_recv()

    ga.forward(0)

    l_wd.wait()

    def dec_block(i):
        blk = jnp.concatenate([wdec[:, i * W:(i + 1) * W], jnp.zeros((128, 128 - W), BF)], axis=1)
        s = slot_of(i // 2 - z)
        WD[c, i % 2, s] = blk
        WDT[s, i % 2] = blk.T

    for i in range(NZ):
        dec_block(i)
    ga.forward(1)
    for i in range(NZ, 2 * NZ):
        dec_block(i)

    def dec_swap(i):
        return to_sister(WD.at[i], WD.at[i], 8)

    dec_swap(c).start()
    drains.append(lambda: dec_swap(c).wait_send())
    comes["dec"] = lambda: dec_swap(oc).wait_recv()
    share_on(0)

    def ring(src, dst, n, own_src, send, d):
        q = plus(p, d, NP)
        if send:
            return copy(src.at[q] if own_src else src, dst.at[p], z_s.at[n, q], z_r.at[n, p], MEM * q + m, tp)
        return copy(dst.at[q], dst.at[q], z_s.at[n, q], z_r.at[n, q], MEM * q + m, tp)

    def far(k):
        return NP // 2 + (k + 1) // 2 * (1 - 2 * (k % 2))

    def ring_start(src, dst, n, own_src, name):
        loop(NP - 1, lambda k: ring(src, dst, n, own_src, True, far(k)).start())
        drains.append(lambda: loop(NP, lambda d: ring(src, dst, n, own_src, True, d).wait_send(), 1))
        comes[name] = lambda: loop(NP, lambda d: ring(src, dst, n, own_src, False, d).wait_recv(), 1)

    got("cot")
    got("sis w0")
    got("last w0")
    bh = mm_nt(CT[0].reshape(RB, 128), WN[0])
    for g in range(1, MEM):
        bh = bh + mm_nt(CT[g].reshape(RB, 128), WN[g])
    BS[...] = folded(bh.reshape(NP, 8, FF)).astype(BF)
    BR[p] = BS[p]
    ring_start(BS, BR, 2, True, "bh sum")
    l_wg.wait()
    l_wu.wait()
    share_out(1)
    share_out(2)

    def pre_part(start, lo, hi):
        pre = start
        for i in range(lo, hi):
            lhs = jnp.concatenate([X[c, :, 0, i].reshape(128, 128), X[c, :, 1, i].reshape(128, 128)], axis=1)
            rhs = jnp.concatenate([WE[0, i].reshape(256, 128), WE[1, i].reshape(256, 128)], axis=1)
            pre = pre + mm(lhs, rhs)
        return pre

    got("bias")
    got("enc")
    got("hit")
    pre = jnp.concatenate([bias2[0, 0:1], bias2[1, 0:1]], axis=1)
    for w, (lo, n) in enumerate(PARTS):
        got("t%d" % w)
        ga.swap(w)
        ga.unpack(c, w)
        pre = pre_part(pre, lo, lo + n)
    act[...] = (pre * jnp.concatenate([hit2[0], hit2[1]], axis=1)).astype(BF)

    got("dec")

    def tsum_out(w, k):
        rows = pl.ds(8 * w, 7)
        e = plus(c, k // 8, 2)
        j = plus(jt, k % 8, 8)
        return copy(S2.at[j, e, rows], R2.at[tp, rows], t_s.at[6 + w, k], t_r.at[6 + w, tp], 2 * z + e,
                    c * 8 + j)

    def tsum_in(w, o):
        rows = pl.ds(8 * w, 7)
        return copy(R2.at[o, rows], R2.at[o, rows], t_s.at[6 + w, o], t_r.at[6 + w, o], 2 * z + ht, o)

    def tsum_drain(w):
        loop(NT, lambda k: tsum_out(w, k).wait_send(), 1)

        @pl.when(ht != c)
        def _():
            tsum_out(w, 0).wait_send()

    def tsum_come(w):
        loop(NT, lambda d: tsum_in(w, plus(tp, d, NT)).wait_recv(), 1)

        @pl.when(ht != c)
        def _():
            tsum_in(w, tp).wait_recv()

    def partial(i):
        rhs = jnp.concatenate([jnp.concatenate([WD[0, e, i], WD[1, e, i]], axis=0) for e in (0, 1)], axis=1)
        both = mm(act[...], rhs)
        return both[:, :128], both[:, 128:]

    for w in (1, 0):
        last = partial(8 * w + 7)
        for k in range(7):
            here = partial(8 * w + k)
            for e in range(2):
                S2[:, e, 8 * w + k] = carry(here[e], last[e], k).astype(BF).reshape(8, 16, 128)
        loop(NT, lambda k: tsum_out(w, k).start(), 1)

        @pl.when(ht != c)
        def _():
            tsum_out(w, 0).start()

        @pl.when(ht == c)
        def _():
            rows = pl.ds(8 * w, 7)
            R2[tp, rows] = S2[jt, c, rows]

        drains.append(functools.partial(tsum_drain, w))
        comes["ts%d" % w] = functools.partial(tsum_come, w)

    actf[c] = act[:, pl.ds(pl.multiple_of(c * 128, 128), 128)]

    def act_swap():
        return to_sister(act.at[:, pl.ds(pl.multiple_of(oc * 128, 128), 128)], actf.at[c], 9)

    act_swap().start()
    drains.append(lambda: act_swap().wait_send())
    comes["act"] = lambda: to_sister(actf.at[oc], actf.at[oc], 9).wait_recv()

    got("bh sum")
    BG[p] = jnp.sum(BR[...].astype(F32), axis=0).astype(BF)
    ring_start(BG.at[p], BG, 3, False, "bh")
    share_on(1)
    share_on(2)
    for w in range(2):
        got("sis0%d" % w)
        ga.unpack(oc, w)
    def z_out(s):
        r = mirror(s)
        return copy(S3.at[s], R3.at[r], z_s.at[4, s], z_r.at[4, r], 2 * z_at(s) + c, tp)

    def z_in(s):
        return copy(R3.at[s], R3.at[s], z_s.at[4, s], z_r.at[4, s], 2 * z_at(s) + c, tp)

    for w in (1, 0):
        got("ts%d" % w)
        terms = [jnp.sum(R2[:, 8 * w + k].astype(F32), axis=0) for k in range(7)]
        terms.append(carried(terms))
        for k in reversed(range(8)):
            S3[8 * w + k] = terms[k].astype(BF)
            if 8 * w + k:
                z_out(8 * w + k).start()
    R3[0] = S3[0]
    drains.append(lambda: loop(NZ, lambda s: z_out(s).wait_send(), 1))
    comes["z sum"] = lambda: loop(NZ, lambda s: z_in(s).wait_recv(), 1)
    for a in (1, 2):
        got("sis w%d" % a)
        got("last w%d" % a)
    for g in range(MEM // 2):
        WGT[g] = WG[2 * g:2 * g + 2].reshape(256, FF).T
        WUT[g] = WU[2 * g:2 * g + 2].reshape(256, FF).T
    got("z sum")
    bias = jnp.concatenate([bdec_ref[...], jnp.zeros((1, 128 - W), F32)], axis=1)
    rc16[...] = (jnp.sum(R3[...].astype(F32), axis=0) + bias).astype(BF)

    def rcopy(d):
        o = plus(tp, d, NT)
        return copy(rc16, RC.at[m, slot], t_s.at[9, o], t_r.at[9, m * TB + slot], MEM * p + mt, o)

    def member(k):
        return plus(m, k // TB, MEM), plus(slot, k % TB, TB)

    def rwait(k):
        g, i = member(k)
        copy(rc16, RC.at[g, i], t_s.at[9, 0], t_r.at[9, g * TB + i], MEM * p + g, m * TB + i).wait_recv()

    loop(NT, lambda d: rcopy(d).start(), 1)

    @pl.when(mt == m)
    def _():
        RC[m, slot] = rc16[...]

    @pl.when(mt != m)
    def _():
        rcopy(0).start()

    def rdrain():
        loop(NT, lambda d: rcopy(d).wait_send(), 1)

        @pl.when(mt != m)
        def _():
            rcopy(0).wait_send()

    drains.append(rdrain)
    loop(MEM * TB, rwait, 1)

    @pl.when(mt != m)
    def _():
        rwait(0)


    def pairs(i):
        return jnp.concatenate([RC[2 * i].reshape(RB, 128), RC[2 * i + 1].reshape(RB, 128)], axis=1)

    gate = mm(pairs(0), WG[0:2].reshape(256, FF))
    up = mm(pairs(0), WU[0:2].reshape(256, FF))
    for i in range(1, MEM // 2):
        gate = gate + mm(pairs(i), WG[2 * i:2 * i + 2].reshape(256, FF))
        up = up + mm(pairs(i), WU[2 * i:2 * i + 2].reshape(256, FF))
    CS[...] = jnp.concatenate([gate.reshape(NP, 8, FF), up.reshape(NP, 8, FF)], axis=1).astype(BF)
    ring_start(CS, CR, 5, True, "gate sum")
    CR[p] = CS[p]
    for h in range(2):
        for i in range(NZ):
            XT[h, i] = X[:, :, h, i].reshape(256, 128).T
    got("act")
    actt[...] = actf[...].reshape(256, 128).T
    got("gate sum")
    AG[p] = jnp.sum(CR[...].astype(F32), axis=0).astype(BF)
    ring_start(AG.at[p], AG, 6, False, "gate")
    got("bh")
    got("gate")

    def cells(i):
        both_ = AG[i].astype(F32)
        gate_, up_ = both_[:8], both_[8:]
        bh_ = unfolded(BG[i].astype(F32))
        gelu_value, slope = gelu_parts(gate_)
        HID[i] = gelu_value * up_
        BGT[i] = bh_ * up_ * slope
        BUP[i] = bh_ * gelu_value

    loop(NP, cells)
    bgate = BGT[...].reshape(RB, FF).astype(BF)
    bup = BUP[...].reshape(RB, FF).astype(BF)
    for g in range(MEM // 2):
        both = (mm(bgate, WGT[g]) + mm(bup, WUT[g])).astype(BF)
        DT[2 * g] = both[:, :128].reshape(TB, 16, 128)
        DT[2 * g + 1] = both[:, 128:].reshape(TB, 16, 128)

    class Sums:
        def __init__(self, src, dst, n):
            self.src, self.dst, self.n = src, dst, n

        def out(self, k):
            g, i = member(k)
            return copy(self.src.at[g, i], self.dst.at[tp], t_s.at[self.n, k], t_r.at[self.n, tp], MEM * p + g,
                        m * TB + i)

        def come(self, d):
            o = plus(tp, d, NT)
            return copy(self.dst.at[o], self.dst.at[o], t_s.at[self.n, 0], t_r.at[self.n, o], MEM * p + mt, o)

        def start(self, name):
            loop(MEM * TB, lambda k: self.out(k).start(), 1)

            @pl.when(mt != m)
            def _():
                self.out(0).start()

            @pl.when(mt == m)
            def _():
                self.dst[tp] = self.src[m, slot]

            def drain():
                loop(MEM * TB, lambda k: self.out(k).wait_send(), 1)

                @pl.when(mt != m)
                def _():
                    self.out(0).wait_send()

            def wait():
                loop(NT, lambda d: self.come(d).wait_recv(), 1)

                @pl.when(mt != m)
                def _():
                    self.come(0).wait_recv()

            drains.append(drain)
            comes[name] = wait

    Sums(DT, RT, 10).start("through")
    hidden = HID[...].reshape(RB, FF).astype(BF)
    for g in range(MEM // 2):
        both = mm(hidden, jnp.concatenate([WN[2 * g], WN[2 * g + 1]], axis=1)).astype(BF)
        DS[2 * g] = both[:, :128].reshape(TB, 16, 128)
        DS[2 * g + 1] = both[:, 128:].reshape(TB, 16, 128)
    base = cpad[tp].astype(F32) + rc16[...].astype(F32) - apad[tp].astype(F32)
    got("through")
    ZB[0] = (base + jnp.sum(RT[...].astype(F32), axis=0)).astype(BF)

    gy = Gather(ZB, ZBP, Y, 1)
    gy.start()
    gy.forward(0)
    gy.forward(1)
    Sums(DS, DR, 11).start("down")

    acc[...] = jnp.zeros_like(acc)

    def back_part(h, w):
        s = acc[h]
        for i in range(PARTS[w][0], sum(PARTS[w])):
            lhs = jnp.concatenate([Y[h, :, 0, i].reshape(128, 128), Y[h, :, 1, i].reshape(128, 128)], axis=1)
            s = s + mm(lhs, WDT[i].reshape(256, 128))
        acc[h] = s

    def leave(src, dst, n):
        cp = pltpu.make_async_copy(src, dst, o_s.at[n])
        cp.start()
        drains.append(cp.wait)

    def dec_part(w):
        for i in range(PARTS[w][0], sum(PARTS[w])):
            rhs = jnp.concatenate([Y[:, :, h, i].reshape(256, 128) for h in range(2)], axis=1)
            both = mm(actt[...], rhs).astype(BF)
            gdec_ref[i, 0] = both[:, :128]
            gdec_ref[i, 1] = both[:, 128:]
        part = pl.ds(*PARTS[w])
        leave(gdec_ref.at[part], gdec_out.at[part], 5 + w)

    def arrived(w):
        got("t%d" % w)
        gy.swap(w)
        gy.unpack(c, w)
        back_part(c, w)

    arrived(0)
    got("sis10")
    gy.unpack(oc, 0)
    back_part(oc, 0)
    dec_part(0)
    got("down")
    out_ref[...] = (rc16[...].astype(F32) + jnp.sum(DR[...].astype(F32), axis=0)).astype(BF)[:, :W]
    arrived(1)
    got("sis11")
    gy.unpack(oc, 1)
    back_part(oc, 1)
    bact = (acc[...].reshape(256, 128) * hit[...]).astype(BF)
    gencb_ref[...] = jnp.sum(bact.astype(F32), axis=0)
    gdecb_ref[...] = jnp.sum(Y[:, :, c, 0].reshape(256, 128).astype(F32), axis=0)[:W]
    actf[...] = bact.reshape(2, 128, 128)

    def enc_grad(k):
        h = k // 4
        first = k % 4 * 4
        four = mm(XT[h, first:first + 4].reshape(512, 256), actf[...].reshape(256, 128)).astype(BF)
        for i in range(4):
            genc_ref[h, first + i] = four[128 * i:128 * i + W]
        part = pl.ds(first, 4)
        leave(genc_ref.at[h, part], genc_out.at[h, part], 7 + k)

    loop(8, enc_grad)
    dec_part(1)
    finish()


def hand_on(out_in, genc_in, gencb_in, gdec_in, gdecb_in, out_ref, genc_ref, gencb_ref, gdec_ref, gdecb_ref):
    z = lax.axis_index("lat") // 2
    out_ref[...] = out_in[...]
    gencb_ref[...] = gencb_in[...]
    gdecb_ref[...] = gdecb_in[...]
    for i in range(2 * NZ):
        s = slot_of(i // 2 - z)
        genc_ref[i * W:(i + 1) * W, :] = genc_in[i % 2, s]
        gdec_ref[:, i * W:(i + 1) * W] = gdec_in[s, i % 2][:, :W]


def step(activations, indices, w_enc, b_enc, w_dec, b_dec, w_gate, w_up, w_down, cotangent):
    vm = pltpu.VMEM
    dma = pltpu.SemaphoreType.DMA
    inside = pl.BlockSpec(memory_space=pltpu.VMEM)
    outside = pl.BlockSpec(memory_space=pl.ANY)
    shapes = (
        jax.ShapeDtypeStruct((16, W), BF),
        jax.ShapeDtypeStruct((2 * NZ * W, 128), BF),
        jax.ShapeDtypeStruct((128,), F32),
        jax.ShapeDtypeStruct((128, 2 * NZ * W), BF),
        jax.ShapeDtypeStruct((W,), F32),
    )
    genc_held = jax.ShapeDtypeStruct((2, NZ, W, 128), BF)
    gdec_held = jax.ShapeDtypeStruct((NZ, 2, 128, 128), BF)
    held = (shapes[0], genc_held, shapes[2], gdec_held, shapes[4])
    results = pl.pallas_call(
        kernel,
        out_shape=held,
        in_specs=[outside] * 10,
        out_specs=[inside, outside, inside, outside, inside],
        scratch_shapes=[
            vm((W, 256), BF),
            vm((64, 256), jnp.int32),
            vm((1, 128), F32),
            vm((1, W), F32),
            vm((W, 256), BF),
            vm(genc_held.shape, BF),
            vm(gdec_held.shape, BF),
            vm((NT, 16, 128), BF),
            vm((NT, 16, 128), BF),
            vm((NZ, 16, 128), BF),
            vm((NZ, 16, 128), BF),
            vm((NZ, 16, 128), BF),
            vm((NZ, 16, 128), BF),
            vm((2, 8, 2, NZ, 16, 128), BF),
            vm((2, 8, 2, NZ, 16, 128), BF),
            vm((2, NZ, 128, 256), BF),
            vm((2, NZ, 2, 128, 128), BF),
            vm((2, 2, NZ, 128, 128), BF),
            vm((NZ, 2, 128, 128), BF),
            vm((256, 128), F32),
            vm((2, 128, 128), F32),
            vm((2, 8, 128), F32),
            vm((128, 256), BF),
            vm((2, 128, 128), BF),
            vm((128, 256), BF),
            vm((2, 128, 128), F32),
            vm((8, 2, NZ, 16, 128), BF),
            vm((NT, NZ, 16, 128), BF),
            vm((NZ, 16, 128), BF),
            vm((NZ, 16, 128), BF),
            vm((16, 128), BF),
            vm((MEM, TB, 16, 128), BF),
            vm((MEM, 128, FF), BF),
            vm((MEM, 128, FF), BF),
            vm((MEM // 2, FF, 256), BF),
            vm((MEM // 2, FF, 256), BF),
            vm((MEM, FF, 128), BF),
            vm((MEM, TB, 16, 128), BF),
            vm((NP, 16, 512), BF),
            vm((NP, 16, 512), BF),
            vm((NP, 16, 512), BF),
            vm((NP, 16, FF), BF),
            vm((NP, 16, FF), BF),
            vm((NP, 16, FF), BF),
            vm((MEM, TB, 16, 128), BF),
            vm((NT, 16, 128), BF),
            vm((MEM, TB, 16, 128), BF),
            vm((NT, 16, 128), BF),
            vm((NP, 8, FF), F32),
            vm((NP, 8, FF), F32),
            vm((NP, 8, FF), F32),
            vm((128, 2 * NZ * W), BF),
            vm((128, FF), BF),
            dma((11,)), dma((11,)),
            dma((7, NZ)), dma((7, NZ)),
            dma((12, NT)), dma((12, NT)),
            dma((4, MEM, 2)), dma((4, MEM)),
            dma((4 + 2 * NZ,)),
            dma((15,)),
        ],
        compiler_params=pltpu.CompilerParams(
            collective_id=1, has_side_effects=True, vmem_limit_bytes=56 * 2**20
        ),
        cost_estimate=pl.CostEstimate(flops=2 * 10**9, bytes_accessed=6 * 10**6, transcendentals=10**5),
        name="sae_step",
    )(
        activations.T, indices.T, w_enc, b_enc.reshape(1, 128), w_dec, b_dec.reshape(1, W),
        w_gate, w_up, w_down.T, cotangent.T,
    )
    return pl.pallas_call(
        hand_on,
        out_shape=shapes,
        in_specs=[inside] * 5,
        out_specs=[inside] * 5,
        compiler_params=pltpu.CompilerParams(vmem_limit_bytes=60 * 2**20),
        name="results",
    )(*results)


def solution(mesh):
    return jax.shard_map(
        step,
        mesh=mesh,
        in_specs=(
            P(None, "lat"),
            P(),
            P(None, ("lat", "tp")),
            P(("lat", "tp")),
            P(("lat", "tp"), None),
            P("lat"),
            P("lat", "tp"),
            P("lat", "tp"),
            P("tp", "lat"),
            P(None, "lat"),
        ),
        out_specs=(
            P("tp", "lat"),
            P(None, ("lat", "tp")),
            P(("lat", "tp")),
            P(("lat", "tp"), None),
            P("lat"),
        ),
        check_vma=False,
    )
```
